32 devices in a mesh: geom: 2 (over y), gx: 4 (over z), gy: 2 (over x), gz: 2 (over core).
Axes of the slice: x: 2, y: 2, z: 4, core: 2. Of those that a mesh axis runs over, the one named last changes fastest.
Arguments:
- features: bfloat16 [20480, 128], P(('geom', 'gx', 'gy', 'gz')), parts along dimension 0, may hold values from -6 to 6
- displacement: float32 [3, 983040], P(None, ('geom', 'gx', 'gy', 'gz')), parts along dimension 1, as said below
- neighbour: int32 [983040], P(('geom', 'gx', 'gy', 'gz')), parts along dimension 0, may hold values from 0 to 2687, as said below
- neighbour_count: int32 [20480], P(('geom', 'gx', 'gy', 'gz')), parts along dimension 0, may hold values from 12 to 48, as said below
- species: int32 [20480], P(('geom', 'gx', 'gy', 'gz')), parts along dimension 0, may hold values from 0 to 99
- exports_x: int32 [32, 2, 640], P(('geom', 'gx', 'gy', 'gz')), parts along dimension 0, may hold values from 0 to 639, as said below
- exports_y: int32 [32, 2, 256], P(('geom', 'gx', 'gy', 'gz')), parts along dimension 0, may hold values from 0 to 639, as said below
- exports_z: int32 [32, 2, 128], P(('geom', 'gx', 'gy', 'gz')), parts along dimension 0, may hold values from 0 to 639, as said below
- face_counts: int32 [32, 6], P(('geom', 'gx', 'gy', 'gz')), parts along dimension 0, may hold values from 1 to 640, as said below
- w_in: bfloat16 [128, 128], replicated, may hold values from -0.5 to 0.5
- w_f1: bfloat16 [50, 128], replicated, may hold values from -1.75 to 1.75
- b_f1: float32 [128], replicated, may hold values from -3 to 3
- w_f2: bfloat16 [128, 128], replicated, may hold values from -0.125 to 0.125
- b_f2: float32 [128], replicated, may hold values from -3 to 3
- w_o1: bfloat16 [128, 128], replicated, may hold values from -0.5 to 0.5
- b_o1: float32 [128], replicated, may hold values from -3 to 3
- w_o2: bfloat16 [128, 128], replicated, may hold values from -0.5 to 0.5
- b_o2: float32 [128], replicated, may hold values from -3 to 3
- w_e1: bfloat16 [128, 64], replicated, may hold values from -0.5 to 0.5
- b_e1: float32 [64], replicated, may hold values from -3 to 3
- w_e2: float32 [64], replicated, may hold values from -1.5 to 1.5
- species_scale: float32 [100], replicated, may hold values from 0.5 to 4
- species_shift: float32 [100], replicated, may hold values from -1 to 1
Outputs:
- energy: float32 [20480], P(('geom', 'gx', 'gy', 'gz')), parts along dimension 0
- forces: float32 [3, 20480], P(None, ('geom', 'gx', 'gy', 'gz')), parts along dimension 1
The draws below stay inside these ranges and needn't reach their ends.
There are 2 independent parts, one for each index of `geom`. The reference program is written for one: setup_inputs(seed, part) draws one part's arguments, and reference() takes and returns one part's arrays. A program takes and returns all parts, laid end to end along the dimension named above; an argument that names none is the same for every part. Nothing has to cross between parts.
Inputs may be any that keep to these rules, and one draw needn't show every extreme that they name: `face_counts`: entry column f is the used length of that face's list: at most 640 for columns 0 and 1, 256 for 2 and 3, 128 for 4 and 5; in every column some domain uses its whole list. `exports_x`: each list row names distinct own atoms. `exports_y`: each list row names distinct own atoms. `exports_z`: each list row names distinct own atoms. `neighbour`: live slots name an own row or a ghost row below the used length of its block; slots beyond the live count hold arbitrary rows. `neighbour_count`: every domain has an atom with all 48 slots live. `displacement`: lengths lie between 0.9 and 4.9.
All inputs are finite; a program needn't handle non-finite values.
Results may differ from the reference program's by a relative error of at most 0.012.
Values may be sent and summed in bfloat16 or wider, within the bound.
A program may use at most 128 MiB of HBM per device.

```python
import math
import jax
import jax.numpy as jnp
import numpy as np
from jax import lax

F = 128
EHID = 64
NSPEC = 100
RBF = 50
NBR = 48
ATOM_DEV = 640
DOMAINS = 16
ATOMS = 10240
PAIRS = 491520
X_GHOSTS = 640
Y_GHOSTS = 256
Z_GHOSTS = 128
GHOSTS = 2048
N_GX = 4
N_GY = 2
N_GZ = 2


def face_caps():
    return jnp.array([X_GHOSTS, X_GHOSTS, Y_GHOSTS, Y_GHOSTS, Z_GHOSTS, Z_GHOSTS], jnp.int32)


def count_table(key):
    caps = face_caps()
    root = jax.random.fold_in(key, 101)
    raw_level = jax.random.randint(jax.random.fold_in(root, 1), (DOMAINS, 6), 0, 1 << 20)
    level = raw_level % caps[None, :] + 1
    squared = (level * level + caps[None, :] - 1) // caps[None, :]
    full_at = jax.random.randint(jax.random.fold_in(root, 2), (6,), 0, DOMAINS)
    domain_ids = jnp.arange(DOMAINS, dtype=jnp.int32)[:, None]
    return jnp.where(domain_ids == full_at[None, :], caps[None, :], squared).astype(jnp.int32)


def received_counts(key):
    table = count_table(key).reshape(N_GX, N_GY, N_GZ, 6)
    stacked = jnp.stack([jnp.roll(table[..., 1], 1, axis=0), jnp.roll(table[..., 0], -1, axis=0), jnp.roll(table[..., 3], 1, axis=1), jnp.roll(table[..., 2], -1, axis=1), jnp.roll(table[..., 5], 1, axis=2), jnp.roll(table[..., 4], -1, axis=2)], axis=-1)
    return stacked.reshape(DOMAINS, 6)


def live_counts(key):
    root = jax.random.fold_in(key, 303)
    counts = jax.random.randint(jax.random.fold_in(root, 1), (DOMAINS, ATOM_DEV), NBR // 4, NBR + 1)
    full_at = jax.random.randint(jax.random.fold_in(root, 2), (DOMAINS, 1), 0, ATOM_DEV)
    atom_ids = jnp.arange(ATOM_DEV, dtype=jnp.int32)[None, :]
    return jnp.where(atom_ids == full_at, NBR, counts).astype(jnp.int32)


def draw_face_counts(key, part):
    return count_table(key)


def draw_neighbour_count(key, part):
    return live_counts(key).reshape(-1)


def draw_neighbour(key, part):
    got_counts = received_counts(key)
    live = live_counts(key)
    offsets = jnp.array([0, X_GHOSTS, 2 * X_GHOSTS, 2 * X_GHOSTS + Y_GHOSTS, 2 * X_GHOSTS + 2 * Y_GHOSTS, 2 * X_GHOSTS + 2 * Y_GHOSTS + Z_GHOSTS], jnp.int32)
    root = jax.random.fold_in(key, 202)
    shape = (DOMAINS, ATOM_DEV, NBR)
    choose_ghost = jax.random.randint(jax.random.fold_in(root, 1), shape, 0, 10)
    block_id = jax.random.randint(jax.random.fold_in(root, 2), shape, 0, 6)
    raw_row = jax.random.randint(jax.random.fold_in(root, 3), shape, 0, 1 << 20)
    local_row = jax.random.randint(jax.random.fold_in(root, 4), shape, 0, ATOM_DEV)
    any_row = jax.random.randint(jax.random.fold_in(root, 5), shape, 0, ATOM_DEV + GHOSTS)
    block_count = jnp.take_along_axis(got_counts, block_id.reshape(DOMAINS, -1), axis=1).reshape(shape)
    ghost_row = ATOM_DEV + jnp.take(offsets, block_id) + raw_row % block_count
    live_row = jnp.where(choose_ghost < 4, ghost_row, local_row)
    slot_ids = jnp.arange(NBR, dtype=jnp.int32)[None, None, :]
    return jnp.where(slot_ids < live[:, :, None], live_row, any_row).astype(jnp.int32).reshape(-1)


def export_lists(key, salt, length):
    keys = jax.random.split(jax.random.fold_in(key, salt), DOMAINS * 2)
    orders = jax.vmap(lambda one_key: jax.random.permutation(one_key, ATOM_DEV))(keys)
    return orders[:, :length].reshape(DOMAINS, 2, length).astype(jnp.int32)


def draw_exports_x(key, part):
    return export_lists(key, 401, X_GHOSTS)


def draw_exports_y(key, part):
    return export_lists(key, 402, Y_GHOSTS)


def draw_exports_z(key, part):
    return export_lists(key, 403, Z_GHOSTS)


def draw_displacement(key, part):
    shape = (PAIRS,)
    radial_u = jax.random.uniform(jax.random.fold_in(key, 501), shape, jnp.float32)
    polar = jax.random.uniform(jax.random.fold_in(key, 502), shape, jnp.float32, -1.0, 1.0)
    azimuth = jax.random.uniform(jax.random.fold_in(key, 503), shape, jnp.float32, 0.0, 2.0 * math.pi)
    radius = 0.9 + 4.0 * radial_u
    side = jnp.sqrt(jnp.maximum(1.0 - polar * polar, 0.0))
    return jnp.stack([radius * side * jnp.cos(azimuth), radius * side * jnp.sin(azimuth), radius * polar]).astype(jnp.float32)


def draw_w_f1(key, part):
    root = jax.random.fold_in(key, 601)
    centres = jnp.arange(RBF, dtype=jnp.float32) * (5.0 / (RBF - 1))
    period = jax.random.uniform(jax.random.fold_in(root, 1), (F,), jnp.float32, 0.8, 2.0)
    phase = jax.random.uniform(jax.random.fold_in(root, 2), (F,), jnp.float32, 0.0, 2.0 * math.pi)
    sign_bit = jax.random.randint(jax.random.fold_in(root, 3), (F,), 0, 2)
    signs = 2.0 * sign_bit.astype(jnp.float32) - 1.0
    level_u = jax.random.uniform(jax.random.fold_in(root, 4), (F,), jnp.float32)
    amplitude = signs * (1.0 + 0.5 * level_u)
    noise = 0.2 * jax.random.normal(jax.random.fold_in(root, 5), (RBF, F), jnp.float32)
    wave = jnp.sin(2.0 * math.pi * centres[:, None] / period[None, :] + phase[None, :])
    values = amplitude[None, :] * wave + noise
    return jnp.clip(values, -1.75, 1.75).astype(jnp.bfloat16)


def set_ends(values, stream_key, least, largest):
    shape = values.shape
    place = [jax.random.randint(jax.random.fold_in(stream_key, axis), (), 0, shape[axis]) for axis in range(len(shape))]
    values = values.at[tuple(place)].set(least)
    longest = shape.index(max(shape))
    place[longest] = (place[longest] + 1) % shape[longest]
    return values.at[tuple(place)].set(largest)


def shard_levels(rng, shape, shards, least, high):
    def one(dim, blocks):
        steps = jax.random.uniform(jax.random.fold_in(jax.random.fold_in(rng, 6), dim), (blocks,), jnp.float32, least / len(shards), high / len(shards))
        return jnp.repeat(jnp.exp(steps), shape[dim] // blocks).reshape((-1,) + (1,) * (len(shape) - dim - 1))

    factor_of = one(*shards[0])
    for cut in shards[1:]:
        factor_of = factor_of * one(*cut)
    return factor_of


def cumulative_ranks(amount, slope):
    portions = [(1 << 20) // math.isqrt(rank ** slope) + 1 for rank in range(1, amount + 1)]
    scale = 1 + sum(portions) // (1 << 30)
    return np.cumsum(np.array([max(1, weight // scale) for weight in portions]))


def ranked(stream_key, extent, amount, slope):
    table = cumulative_ranks(amount, slope)
    ticket = jax.random.randint(jax.random.fold_in(stream_key, 1), extent, 0, int(table[amount - 1]))
    rank = jnp.searchsorted(jnp.asarray(table, jnp.int32), ticket, side="right")
    return jax.random.permutation(jax.random.fold_in(stream_key, 2), amount)[rank].astype(jnp.int32)


def scatter_about(stream_key, extent, scale, most, cuts=(), kind=jnp.bfloat16):
    entries = jax.random.normal(stream_key, extent, jnp.float32) * scale
    if len(cuts) > 0:
        entries = shard_levels(stream_key, extent, cuts, -0.22, 0.18) * entries
    return jnp.clip(entries, min=-most, max=most).astype(kind)


def setup_inputs(seed: int = 0, part: int = 0) -> dict:
    seeds = jax.random.split(jax.random.key(seed), 24)
    own_keys = jax.random.split(jax.random.fold_in(seeds[23], part), 24)
    return {
        "features": scatter_about(own_keys[0], (ATOMS, F), 1.0, 6.0, ((0, 16),)),
        "displacement": draw_displacement(jax.random.fold_in(jax.random.fold_in(seeds[23], part), 71), part),
        "neighbour": draw_neighbour(jax.random.fold_in(jax.random.fold_in(seeds[23], part), 71), part),
        "neighbour_count": draw_neighbour_count(jax.random.fold_in(jax.random.fold_in(seeds[23], part), 71), part),
        "species": set_ends(ranked(own_keys[4], (ATOMS,), NSPEC, 2), jax.random.fold_in(own_keys[4], 3), 0, NSPEC - 1).astype(jnp.int32),
        "exports_x": draw_exports_x(jax.random.fold_in(jax.random.fold_in(seeds[23], part), 71), part),
        "exports_y": draw_exports_y(jax.random.fold_in(jax.random.fold_in(seeds[23], part), 71), part),
        "exports_z": draw_exports_z(jax.random.fold_in(jax.random.fold_in(seeds[23], part), 71), part),
        "face_counts": draw_face_counts(jax.random.fold_in(jax.random.fold_in(seeds[23], part), 71), part),
        "w_in": scatter_about(seeds[9], (F, F), F ** -0.5, 0.5),
        "w_f1": draw_w_f1(jax.random.fold_in(seeds[23], 71), part),
        "b_f1": scatter_about(seeds[11], (F,), 1.0, 3.0, (), jnp.float32),
        "w_f2": scatter_about(seeds[12], (F, F), (16 * F) ** -0.5, 0.125),
        "b_f2": scatter_about(seeds[13], (F,), 0.5, 3.0, (), jnp.float32),
        "w_o1": scatter_about(seeds[14], (F, F), F ** -0.5, 0.5),
        "b_o1": scatter_about(seeds[15], (F,), 0.5, 3.0, (), jnp.float32),
        "w_o2": scatter_about(seeds[16], (F, F), F ** -0.5, 0.5),
        "b_o2": scatter_about(seeds[17], (F,), 0.5, 3.0, (), jnp.float32),
        "w_e1": scatter_about(seeds[18], (F, EHID), F ** -0.5, 0.5),
        "b_e1": scatter_about(seeds[19], (EHID,), 0.5, 3.0, (), jnp.float32),
        "w_e2": scatter_about(seeds[20], (EHID,), (EHID // 4) ** -0.5, 1.5, (), jnp.float32),
        "species_scale": jnp.clip(jnp.exp(jax.random.uniform(seeds[21], (NSPEC,), jnp.float32, math.log(0.5), math.log(4.0))), 0.5, 4.0),
        "species_shift": jnp.clip(jax.random.uniform(seeds[22], (NSPEC,), jnp.float32, -1.0, 1.0), -1.0, 1.0),
    }


GAMMA = 10.0
CUTOFF = 5.0
LOG_TWO = math.log(2.0)

def shifted_softplus(value):
    return jax.nn.softplus(value) - LOG_TWO

def block_terms(table, feat_rows, disp_rows, index_rows, count_rows, scale_rows, shift_rows, weights):
    w_f1, b_f1, w_f2, b_f2, w_o1, b_o1, w_o2, b_o2, w_e1, b_e1, w_e2 = weights
    row_count = feat_rows.shape[0]
    slot_count = index_rows.shape[0] // row_count
    width = feat_rows.shape[1]
    radial = w_f1.shape[0]
    distance = jnp.sqrt(lax.optimization_barrier(jnp.sum(disp_rows * disp_rows, axis=0)))
    centres = jnp.arange(radial, dtype=jnp.float32) * (CUTOFF / (radial - 1))
    offset = distance[None, :] - centres[:, None]
    basis_vals = jnp.exp(-GAMMA * offset * offset)
    basis_slope = -2.0 * GAMMA * offset * basis_vals
    phase_arg = jnp.pi * distance / CUTOFF
    envelope = 0.5 * (jnp.cos(phase_arg) + 1.0)
    envelope_slope = -0.5 * jnp.pi / CUTOFF * jnp.sin(phase_arg)
    slot_index = lax.broadcasted_iota(jnp.int32, (row_count, slot_count), 1)
    live_mask = (slot_index < count_rows[:, None]).astype(jnp.float32).reshape(-1)
    pre_act = lax.dot_general(basis_vals.astype(jnp.bfloat16), w_f1, (((0,), (0,)), ((), ())), preferred_element_type=jnp.float32) + b_f1
    hidden = shifted_softplus(pre_act).astype(jnp.bfloat16)
    filter_out = jnp.dot(hidden, w_f2, preferred_element_type=jnp.float32) + b_f2
    pair_weight = filter_out * (envelope * live_mask)[:, None]
    neighbour_rows = table[index_rows].astype(jnp.float32)
    message = lax.optimization_barrier(jnp.sum((neighbour_rows * pair_weight).reshape(row_count, slot_count, width), axis=1))
    out_pre = jnp.dot(message.astype(jnp.bfloat16), w_o1, preferred_element_type=jnp.float32) + b_o1
    out_mid = shifted_softplus(out_pre).astype(jnp.bfloat16)
    updated = feat_rows.astype(jnp.float32) + jnp.dot(out_mid, w_o2, preferred_element_type=jnp.float32) + b_o2
    energy_pre = jnp.dot(updated.astype(jnp.bfloat16), w_e1, preferred_element_type=jnp.float32) + b_e1
    energy = scale_rows * lax.optimization_barrier(jnp.sum(shifted_softplus(energy_pre) * w_e2[None, :], axis=1)) + shift_rows
    grad_head = (scale_rows[:, None] * w_e2[None, :] * jax.nn.sigmoid(energy_pre)).astype(jnp.bfloat16)
    grad_update = jnp.dot(grad_head, w_e1.T, preferred_element_type=jnp.float32).astype(jnp.bfloat16)
    grad_mid = (jnp.dot(grad_update, w_o2.T, preferred_element_type=jnp.float32) * jax.nn.sigmoid(out_pre)).astype(jnp.bfloat16)
    grad_message = jnp.dot(grad_mid, w_o1.T, preferred_element_type=jnp.float32)
    pair_grad = (grad_message[:, None, :] * neighbour_rows.reshape(row_count, slot_count, width)).reshape(-1, width) * live_mask[:, None]
    grad_filter = (pair_grad * envelope[:, None]).astype(jnp.bfloat16)
    grad_pre = (jnp.dot(grad_filter, w_f2.T, preferred_element_type=jnp.float32) * jax.nn.sigmoid(pre_act)).astype(jnp.bfloat16)
    grad_basis = lax.dot_general(w_f1, grad_pre, (((1,), (1,)), ((), ())), preferred_element_type=jnp.float32)
    grad_dist = lax.optimization_barrier(jnp.sum(grad_basis * basis_slope, axis=0)) + lax.optimization_barrier(jnp.sum(pair_grad * filter_out, axis=1)) * envelope_slope
    pair_force = disp_rows * (grad_dist / distance)[None, :]
    return (energy, pair_force)

def reference(features, displacement, neighbour, neighbour_count, species, exports_x, exports_y, exports_z, face_counts, w_in, w_f1, b_f1, w_f2, b_f2, w_o1, b_o1, w_o2, b_o2, w_e1, b_e1, w_e2, species_scale, species_shift):
    domains = N_GX * N_GY * N_GZ
    grid = (N_GX, N_GY, N_GZ)
    width = features.shape[1]
    x_local = jnp.dot(features, w_in, preferred_element_type=jnp.float32).astype(jnp.bfloat16).reshape(domains, ATOM_DEV, width)

    def export_rows(lists, column):
        picked = jax.vmap(lambda rows_all, index_row: rows_all[index_row])(x_local, lists)
        kept_mask = jnp.arange(lists.shape[1], dtype=jnp.int32)[None, :] < face_counts[:, column][:, None]
        picked = jnp.where(kept_mask[:, :, None], picked, jnp.zeros_like(picked))
        return picked.reshape(grid + picked.shape[1:])
    blocks_in = [jnp.roll(export_rows(exports_x[:, 1], 1), 1, axis=0), jnp.roll(export_rows(exports_x[:, 0], 0), -1, axis=0), jnp.roll(export_rows(exports_y[:, 1], 3), 1, axis=1), jnp.roll(export_rows(exports_y[:, 0], 2), -1, axis=1), jnp.roll(export_rows(exports_z[:, 1], 5), 1, axis=2), jnp.roll(export_rows(exports_z[:, 0], 4), -1, axis=2)]
    ghost_rows = jnp.concatenate([piece.reshape(domains, -1, width) for piece in blocks_in], axis=1)
    tables = jnp.concatenate([x_local, ghost_rows], axis=1)
    scale_all = species_scale[species]
    shift_all = species_shift[species]
    weights = (w_f1, b_f1, w_f2, b_f2, w_o1, b_o1, w_o2, b_o2, w_e1, b_e1, w_e2)

    def one_domain(pieces):
        table, feat_rows, disp_rows, index_rows, count_rows, scale_rows, shift_rows = pieces
        energy, pair_force = block_terms(table, feat_rows, disp_rows, index_rows, count_rows, scale_rows, shift_rows, weights)
        own_force = lax.optimization_barrier(jnp.sum(pair_force.reshape(3, ATOM_DEV, -1), axis=2))
        spread = jnp.zeros((3, table.shape[0]), jnp.float32).at[:, index_rows].add(-pair_force)
        return (energy, own_force + spread[:, :ATOM_DEV], spread[:, ATOM_DEV:])
    energy, forces, ghost_force = lax.map(one_domain, (tables, features.reshape(domains, ATOM_DEV, width), displacement.reshape(3, domains, -1).transpose(1, 0, 2), neighbour.reshape(domains, -1), neighbour_count.reshape(domains, -1), scale_all.reshape(domains, -1), shift_all.reshape(domains, -1)))
    ghost_force = ghost_force.reshape(grid + (3, -1))

    def return_block(forces, start, length, by, axis, lists, column):
        piece = jnp.roll(ghost_force[..., start:start + length], by, axis=axis).reshape(domains, 3, length)
        kept_mask = jnp.arange(length, dtype=jnp.int32)[None, :] < face_counts[:, column][:, None]
        piece = jnp.where(kept_mask[:, None, :], piece, jnp.zeros_like(piece))
        return jax.vmap(lambda total, index_row, values: total.at[:, index_row].add(values))(forces, lists, piece)
    start_y = 2 * X_GHOSTS
    start_z = 2 * X_GHOSTS + 2 * Y_GHOSTS
    forces = return_block(forces, 0, X_GHOSTS, -1, 0, exports_x[:, 1], 1)
    forces = return_block(forces, X_GHOSTS, X_GHOSTS, 1, 0, exports_x[:, 0], 0)
    forces = return_block(forces, start_y, Y_GHOSTS, -1, 1, exports_y[:, 1], 3)
    forces = return_block(forces, start_y + Y_GHOSTS, Y_GHOSTS, 1, 1, exports_y[:, 0], 2)
    forces = return_block(forces, start_z, Z_GHOSTS, -1, 2, exports_z[:, 1], 5)
    forces = return_block(forces, start_z + Z_GHOSTS, Z_GHOSTS, 1, 2, exports_z[:, 0], 4)
    return (energy.reshape(-1), forces.transpose(1, 0, 2).reshape(3, -1))
```

```python
import math

import jax
import jax.numpy as jnp
from jax import lax
from jax.experimental import pallas as pl
from jax.experimental.pallas import tpu as pltpu
from jax.sharding import PartitionSpec as P

GAMMA = 10.0
CUTOFF = 5.0
LOG_TWO = math.log(2.0)
LOG2E = 1.0 / LOG_TWO
LANES = 128
UNROLL = 4
CHUNK = 256
RADIAL_ROWS = 64
GROUP_ROWS = 32

BF16 = jnp.bfloat16
F32 = jnp.float32


def dot(a, b):
    return jnp.dot(a, b, preferred_element_type=F32)


def dot_nt(a, b):
    return lax.dot_general(a, b, (((1,), (1,)), ((), ())), preferred_element_type=F32)


def split3(value):
    high = value.astype(BF16)
    rest = value - high.astype(F32)
    middle = rest.astype(BF16)
    low = (rest - middle.astype(F32)).astype(BF16)
    return high, middle, low


def softplus_of(value):
    return jnp.maximum(value, 0.0) + jnp.log(1.0 + jnp.exp(-jnp.abs(value)))


def sigmoid_of(value):
    return 1.0 / (1.0 + jnp.exp(-value))


def flip(weight):
    return weight.astype(F32).T.astype(BF16)


def pair_kernel(
    disp_ref,
    index_ref,
    count_ref,
    species_ref,
    scale_ref,
    shift_ref,
    feat_ref,
    table_ref,
    w1_ref,
    b1_ref,
    w2_ref,
    wo1_ref,
    wo2_ref,
    we1_ref,
    bf2_ref,
    bo1_ref,
    bo2_ref,
    be1_ref,
    w_e2_ref,
    energy_ref,
    own_ref,
    spread_ref,
    dist_ref,
    env_ref,
    row_ref,
    near_ref,
    far_ref,
    disp3_ref,
    msg_ref,
    gm_ref,
    own3_ref,
    xj_ref,
    prod_ref,
    sig_ref,
    slope_ref,
    hid_a_ref,
    hid_b_ref,
    filt_a_ref,
    filt_b_ref,
    found_a_ref,
    found_b_ref,
    back_a_ref,
    back_b_ref,
    total_ref,
):
    slots, atoms = index_ref.shape
    width = feat_ref.shape[1]
    tiles = atoms // LANES
    steps = slots // UNROLL
    span = UNROLL * LANES
    radial = w1_ref.shape[0]
    table_rows = table_ref.shape[1]
    idle = tiles * steps

    atom_row = lax.broadcasted_iota(jnp.int32, (1, atoms), 1)
    atom_col = lax.broadcasted_iota(jnp.int32, (atoms, 1), 0)
    count_row = count_ref[...].reshape(1, atoms)
    key_row = (count_row * atoms - atom_row).astype(F32)
    count_col = jnp.broadcast_to(count_row.astype(F32), (128, atoms)).T[:, 0:1]
    key_col = count_col * float(atoms) - atom_col.astype(F32)
    rank_col = jnp.sum(jnp.where(key_row > key_col, 1.0, 0.0), axis=1, keepdims=True)
    perm = jnp.where(rank_col == atom_row.astype(F32), 1.0, 0.0).astype(BF16)

    def sort_exact(value):
        high, middle, low = split3(value)
        return dot(high, perm) + dot(middle, perm) + dot(low, perm)

    def unsort_exact(value):
        high, middle, low = split3(value)
        return dot_nt(high, perm) + dot_nt(middle, perm) + dot_nt(low, perm)

    def put(ref, value):
        for tile in range(tiles):
            for s in range(steps):
                ref[tile * steps + s] = value[
                    s * UNROLL : (s + 1) * UNROLL, tile * LANES : (tile + 1) * LANES
                ]
        ref[idle] = jnp.zeros((UNROLL, LANES), F32)

    disp = sort_exact(disp_ref[...])
    index = index_ref[...]
    index_high = dot((index >> 7).astype(F32).astype(BF16), perm)
    index_low = dot((index & 127).astype(F32).astype(BF16), perm)
    put(row_ref, index_high * 128.0 + index_low)
    counts = dot(
        jnp.broadcast_to(count_row, (8, atoms)).astype(F32).astype(BF16), perm
    )[0:1]
    kinds = scale_ref.shape[0]
    kind_ids = lax.broadcasted_iota(jnp.int32, (kinds, 1), 0)
    kind_pick = jnp.where(kind_ids == species_ref[...].reshape(1, atoms), 1.0, 0.0).astype(BF16)
    pair_of = jnp.concatenate(
        [
            jnp.broadcast_to(scale_ref[...].reshape(1, kinds), (8, kinds)),
            jnp.broadcast_to(shift_ref[...].reshape(1, kinds), (8, kinds)),
        ],
        axis=0,
    )
    atom_vals = sort_exact(sum(dot(part, kind_pick) for part in split3(pair_of)))
    scale = atom_vals[0:1]
    shift = atom_vals[8:9]
    feat = dot(feat_ref[...].astype(F32).T.astype(BF16), perm)

    dx = disp[0:slots]
    dy = disp[slots : 2 * slots]
    dz = disp[2 * slots : 3 * slots]
    squared = dx * dx + dy * dy + dz * dz
    distance = jnp.sqrt(squared)
    put(dist_ref, distance)
    slot_ids = lax.broadcasted_iota(jnp.int32, (slots, 1), 0).astype(F32)
    live = jnp.where(slot_ids < counts, 1.0, 0.0)
    y = (math.pi / CUTOFF) * distance - 0.5 * math.pi
    y2 = y * y
    sin_y = y * (
        1.0
        + y2
        * (
            -1.0 / 6
            + y2 * (1.0 / 120 + y2 * (-1.0 / 5040 + y2 * (1.0 / 362880 - y2 * (1.0 / 39916800))))
        )
    )
    envelope = (0.5 - 0.5 * sin_y) * live
    put(env_ref, envelope)
    cos_y = 1.0 + y2 * (
        -0.5
        + y2
        * (
            1.0 / 24
            + y2
            * (
                -1.0 / 720
                + y2 * (1.0 / 40320 + y2 * (-1.0 / 3628800 + y2 * (1.0 / 479001600)))
            )
        )
    )
    inverse = live / distance
    put(near_ref, envelope * (-2.0 * GAMMA) * inverse)
    put(far_ref, (-0.5 * math.pi / CUTOFF * LOG_TWO) * cos_y * inverse)
    put(disp3_ref.at[0], dx)
    put(disp3_ref.at[1], dy)
    put(disp3_ref.at[2], dz)

    bias = b1_ref[...].reshape(1, width)
    bias_high = bias.astype(BF16).astype(F32)
    bias_middle = (bias - bias_high).astype(BF16).astype(F32)
    w1 = jnp.concatenate(
        [
            w1_ref[...].astype(F32),
            bias_high,
            bias_middle,
            bias - bias_high - bias_middle,
            jnp.zeros((RADIAL_ROWS - radial - 3, width), F32),
        ],
        axis=0,
    )
    w1t = w1.T.astype(BF16)
    radial_col = lax.broadcasted_iota(jnp.int32, (RADIAL_ROWS, 1), 0)
    w1_back = jnp.where(radial_col < radial, w1, 0.0).astype(BF16)
    mu = radial_col.astype(F32) * (CUTOFF / (radial - 1))
    sharp = jnp.where(radial_col < radial, -GAMMA * LOG2E, 0.0)
    w2 = w2_ref[...]
    w2t = flip(w2)

    def column(ref):
        size = ref.shape[0]
        return jnp.broadcast_to(ref[...].reshape(1, size), (128, size)).T[:, 0:1]

    b_f2 = column(bf2_ref) * LOG2E
    b_o1 = column(bo1_ref)
    b_o2 = column(bo2_ref)
    b_e1 = column(be1_ref)
    w_e2 = column(w_e2_ref)

    def lane_row(ref, at):
        return jnp.concatenate([ref[at, u : u + 1, :] for u in range(UNROLL)], axis=1)

    ends = []
    items = jnp.zeros((), jnp.int32)
    for tile in range(tiles):
        most = jnp.max(counts[:, tile * LANES : (tile + 1) * LANES]).astype(jnp.int32)
        items = items + (most + (UNROLL - 1)) // UNROLL
        ends.append(items)
    rounds = (items + 1) // 2

    def place(item):
        tile = jnp.zeros((), jnp.int32)
        first = jnp.zeros((), jnp.int32)
        for end in ends[:-1]:
            past = item >= end
            tile = tile + past.astype(jnp.int32)
            first = jnp.where(past, end, first)
        at = jnp.where((item >= 0) & (item < items), tile * steps + item - first, idle)
        return tile, at

    def gather(row):
        parts = []
        for start in range(0, table_rows, CHUNK):
            size = min(CHUNK, table_rows - start)
            spot = jnp.broadcast_to(row - float(start), (16, span)).astype(BF16)
            lanes = lax.broadcasted_iota(jnp.int32, (16, span), 0).astype(F32)
            for b in range(size // 16):
                ids = (lanes + float(16 * b)).astype(BF16)
                parts.append(
                    jnp.where(ids == spot, jnp.ones((), BF16), jnp.zeros((), BF16))
                )
        return dot(table_ref[...], jnp.concatenate(parts, axis=0))

    def radial_dot(at):
        offset = lane_row(dist_ref, at) - mu
        basis = jnp.exp2(sharp * (offset * offset))
        return (offset * basis).astype(BF16), dot(w1t, basis.astype(BF16))

    def activate(pre):
        grown = jnp.exp2(pre * LOG2E)
        total = 1.0 + grown
        sig = (grown * pl.reciprocal(total, approx=True)).astype(BF16)
        return sig, (jnp.log2(total) - 1.0).astype(BF16)

    def begin(item, hid_ref):
        slope, pre = radial_dot(place(item)[1])
        slope_ref[item + 1] = slope
        sig, hidden = activate(pre)
        sig_ref[item + 1] = sig
        hid_ref[...] = hidden

    def finish(item, filt_ref, found_ref):
        tile, at = place(item)
        prod = found_ref[...] * filt_ref[...]
        prod_ref[item + 1] = prod.astype(BF16)
        weighted = prod * lane_row(env_ref, at)
        part = msg_ref[tile]
        for u in range(UNROLL):
            part = part + weighted[:, u * LANES : (u + 1) * LANES]
        msg_ref[tile] = part

    def forward(item, hid_ref, next_ref, filt_ref, found_ref, last_filt_ref, last_found_ref):
        filt = dot(w2t, hid_ref[...]) + b_f2
        slope, pre = radial_dot(place(item + 1)[1])
        slope_ref[item + 2] = slope
        found = gather(lane_row(row_ref, place(item)[1]))
        sig, hidden = activate(pre)
        sig_ref[item + 2] = sig
        next_ref[...] = hidden
        finish(item - 1, last_filt_ref, last_found_ref)
        filt_ref[...] = filt
        found_ref[...] = found
        xj_ref[item + 1] = found.astype(BF16)

    msg_ref[...] = jnp.zeros_like(msg_ref)
    filt_b_ref[...] = jnp.zeros_like(filt_b_ref)
    found_b_ref[...] = jnp.zeros_like(found_b_ref)
    begin(jnp.zeros((), jnp.int32), hid_a_ref)

    def forward_round(turn, carry):
        item = 2 * turn
        forward(item, hid_a_ref, hid_b_ref, filt_a_ref, found_a_ref, filt_b_ref, found_b_ref)
        forward(item + 1, hid_b_ref, hid_a_ref, filt_b_ref, found_b_ref, filt_a_ref, found_a_ref)
        return carry

    lax.fori_loop(0, rounds, forward_round, 0)
    finish(2 * rounds - 1, filt_b_ref, found_b_ref)

    wo1 = wo1_ref[...]
    wo2 = wo2_ref[...]
    we1 = we1_ref[...]
    message = jnp.concatenate([msg_ref[t] for t in range(tiles)], axis=1)
    message = (message * LOG_TWO).astype(BF16)
    out_pre = dot(flip(wo1), message) + b_o1
    out_mid = (softplus_of(out_pre) - LOG_TWO).astype(BF16)
    updated = (feat + dot(flip(wo2), out_mid) + b_o2).astype(BF16)
    energy_pre = dot(we1, updated) + b_e1
    soft = softplus_of(energy_pre) - LOG_TWO
    energy = scale * jnp.sum(soft * w_e2, axis=0, keepdims=True) + shift
    grad_head = (scale * w_e2 * sigmoid_of(energy_pre)).astype(BF16)
    grad_update = dot(flip(we1), grad_head).astype(BF16)
    grad_mid = (dot(wo2, grad_update) * sigmoid_of(out_pre)).astype(BF16)
    grad_message = dot(wo1, grad_mid)
    for tile in range(tiles):
        gm_ref[tile] = grad_message[:, tile * LANES : (tile + 1) * LANES]

    total_ref[...] = jnp.zeros_like(total_ref)
    own3_ref[...] = jnp.zeros_like(own3_ref)
    back_b_ref[...] = jnp.zeros_like(back_b_ref)
    prod_ref[0] = jnp.zeros((width, span), BF16)
    slope_ref[0] = jnp.zeros((RADIAL_ROWS, span), BF16)

    def settle(item, back_ref):
        tile, at = place(item)
        grad_basis = dot(w1_back, back_ref[...])
        grad_wide = jnp.concatenate([gm_ref[tile]] * UNROLL, axis=1)
        s1 = jnp.sum(grad_basis * slope_ref[item + 1].astype(F32), axis=0, keepdims=True)
        s2 = jnp.sum(grad_wide * prod_ref[item + 1].astype(F32), axis=0, keepdims=True)
        ratio = s1 * lane_row(near_ref, at) + s2 * lane_row(far_ref, at)
        row = lane_row(row_ref, at)
        high = jnp.floor(row * (1.0 / 128))
        low = row - high * 128.0
        wide = (16, span)
        high_b = jnp.broadcast_to(high, wide).astype(BF16)
        low_b = jnp.broadcast_to(low, wide).astype(BF16)
        lanes = lax.broadcasted_iota(jnp.int32, wide, 0).astype(F32)
        ids = [(lanes + float(16 * b)).astype(BF16) for b in range(8)]
        lower = jnp.concatenate(
            [jnp.where(one == low_b, jnp.ones((), BF16), jnp.zeros((), BF16)) for one in ids],
            axis=0,
        )
        here = [ids[b] == high_b for b in range(GROUP_ROWS // 16)]
        placed = []
        for c in range(3):
            force = ratio * lane_row(disp3_ref.at[c], at)
            part = own3_ref[tile, c : c + 1, :]
            for u in range(UNROLL):
                part = part + force[:, u * LANES : (u + 1) * LANES]
            own3_ref[tile, c : c + 1, :] = part
            minus = jnp.broadcast_to(-force, wide).astype(BF16)
            placed += [jnp.where(mask, minus, jnp.zeros((), BF16)) for mask in here]
        total_ref[...] = total_ref[...] + dot_nt(jnp.concatenate(placed, axis=0), lower)

    def backward(item, back_ref, last_ref):
        tile, at = place(item)
        grad_b = gm_ref[tile].astype(BF16)
        grad_b_wide = jnp.concatenate([grad_b] * UNROLL, axis=1)
        mixed = dot(w2, grad_b_wide * xj_ref[item + 1])
        settle(item - 1, last_ref)
        back_ref[...] = (mixed * sig_ref[item + 1].astype(F32)).astype(BF16)

    def backward_round(turn, carry):
        item = 2 * turn
        backward(item, back_a_ref, back_b_ref)
        backward(item + 1, back_b_ref, back_a_ref)
        return carry

    lax.fori_loop(0, rounds, backward_round, 0)
    settle(2 * rounds - 1, back_b_ref)

    own = jnp.concatenate(
        [
            jnp.concatenate([own3_ref[t, 0:3, :] for t in range(tiles)], axis=1),
            energy,
            jnp.zeros((4, atoms), F32),
        ],
        axis=0,
    )
    plain = unsort_exact(own)
    own_ref[...] = plain
    energy_ref[...] = plain[3:4].reshape(atoms)
    spread_ref[...] = jnp.zeros_like(spread_ref)
    for c in range(3):
        spread_ref[:, c, :] = total_ref[c * GROUP_ROWS : c * GROUP_ROWS + spread_ref.shape[0]]


def neighbours():
    found = []
    for axis in ("gx", "gy", "gz"):
        size = lax.axis_size(axis)
        place = lax.axis_index(axis)
        found.append({axis: lax.rem(place + 1, size)})
        found.append({axis: lax.rem(place + size - 1, size)})
    return found


def greet(found):
    barrier = pltpu.get_barrier_semaphore()
    for device in found:
        pl.semaphore_signal(
            barrier, inc=1, device_id=device, device_id_type=pl.DeviceIdType.MESH
        )
    pl.semaphore_wait(barrier, len(found))


def picker(list_row, used, atoms):
    lanes = lax.broadcasted_iota(jnp.int32, list_row.shape, 1)
    names = jnp.where(lanes < used, list_row, -1).astype(F32)
    ids = lax.broadcasted_iota(jnp.int32, (atoms, 1), 0).astype(F32)
    return jnp.where(ids == names, 1.0, 0.0).astype(BF16)


FACES = ((0, 1, 1, 0), (0, 0, 0, 1), (1, 1, 3, 2), (1, 0, 2, 3), (2, 1, 5, 4), (2, 0, 4, 5))


def send_kernel(
    feat_ref, w_ref, ex_ref, ey_ref, ez_ref, used_ref, table_ref, stage_ref, send_sem, recv_sem
):
    atoms = feat_ref.shape[0]
    lists = (ex_ref, ey_ref, ez_ref)
    found = neighbours()
    x = dot(feat_ref[...], w_ref[...])
    x_t = x.T.astype(BF16)
    used = used_ref[...]
    greet(found)
    copies = []
    start = 0
    for n, (dim, side, column, to) in enumerate(FACES):
        length = lists[dim].shape[1]
        pick = picker(lists[dim][side : side + 1, :], used[:, column : column + 1], atoms)
        stage_ref[:, start : start + length] = dot(x_t, pick).astype(BF16)
        copy = pltpu.make_async_remote_copy(
            src_ref=stage_ref.at[:, pl.ds(start, length)],
            dst_ref=table_ref.at[:, pl.ds(atoms + start, length)],
            send_sem=send_sem.at[n],
            recv_sem=recv_sem.at[n],
            device_id=found[to],
            device_id_type=pl.DeviceIdType.MESH,
        )
        copy.start()
        copies.append(copy)
        start += length
    table_ref[:, 0:atoms] = x_t
    for copy in copies:
        copy.wait()


def return_kernel(
    own_ref,
    spread_ref,
    ex_ref,
    ey_ref,
    ez_ref,
    used_ref,
    force_ref,
    land_ref,
    send_sem,
    recv_sem,
):
    atoms = force_ref.shape[1]
    lists = (ex_ref, ey_ref, ez_ref)
    found = neighbours()
    greet(found)
    copies = []
    group = atoms // 128
    start = 0
    for n, (dim, side, column, to) in enumerate(FACES):
        length = lists[dim].shape[1] // 128
        copy = pltpu.make_async_remote_copy(
            src_ref=spread_ref.at[pl.ds(group + start, length)],
            dst_ref=land_ref.at[pl.ds(start, length)],
            send_sem=send_sem.at[n],
            recv_sem=recv_sem.at[n],
            device_id=found[to ^ 1],
            device_id_type=pl.DeviceIdType.MESH,
        )
        copy.start()
        copies.append(copy)
        start += length
    total = own_ref[...] + jnp.concatenate([spread_ref[h] for h in range(group)], axis=1)
    used = used_ref[...]
    start = 0
    for n, (dim, side, column, to) in enumerate(FACES):
        length = lists[dim].shape[1] // 128
        pick = picker(lists[dim][side : side + 1, :], used[:, column : column + 1], atoms)
        copies[n].wait()
        values = jnp.concatenate([land_ref[start + h] for h in range(length)], axis=1)
        high, middle, low = split3(values)
        total = total + dot_nt(high, pick) + dot_nt(middle, pick) + dot_nt(low, pick)
        start += length
    force_ref[...] = total[0:3]


def body(
    features,
    displacement,
    neighbour,
    neighbour_count,
    species,
    exports_x,
    exports_y,
    exports_z,
    face_counts,
    w_in,
    w_f1,
    b_f1,
    w_f2,
    b_f2,
    w_o1,
    b_o1,
    w_o2,
    b_o2,
    w_e1,
    b_e1,
    w_e2,
    species_scale,
    species_shift,
):
    atom_rows, width = features.shape
    slot_count = neighbour.shape[0] // atom_rows
    used_counts = face_counts[0]
    vmem = pl.BlockSpec(memory_space=pltpu.VMEM)
    lists = (exports_x[0], exports_y[0], exports_z[0])
    ghost_rows = sum(2 * one.shape[1] for one in lists)
    table_rows = atom_rows + ghost_rows
    table_t = pl.pallas_call(
        send_kernel,
        out_shape=jax.ShapeDtypeStruct((width, table_rows), BF16),
        in_specs=[vmem] * 6,
        out_specs=vmem,
        scratch_shapes=[
            pltpu.VMEM((width, ghost_rows), BF16),
            pltpu.SemaphoreType.DMA((6,)),
            pltpu.SemaphoreType.DMA((6,)),
        ],
        compiler_params=pltpu.CompilerParams(
            collective_id=0, has_side_effects=True, vmem_limit_bytes=32 * 1024 * 1024
        ),
    )(features, w_in, *lists, face_counts)
    disp_t = (
        displacement.reshape(3, atom_rows, slot_count).transpose(0, 2, 1).reshape(-1, atom_rows)
    )
    index_t = neighbour.reshape(atom_rows, slot_count).T
    steps = slot_count // UNROLL * (atom_rows // LANES)
    tiles = atom_rows // LANES
    groups = table_rows // 128
    span = UNROLL * LANES
    energy, own_force, spread = pl.pallas_call(
        pair_kernel,
        out_shape=(
            jax.ShapeDtypeStruct((atom_rows,), F32),
            jax.ShapeDtypeStruct((8, atom_rows), F32),
            jax.ShapeDtypeStruct((groups, 8, 128), F32),
        ),
        in_specs=[vmem] * 19,
        out_specs=(vmem, vmem, vmem),
        scratch_shapes=[pltpu.VMEM((steps + 1, UNROLL, LANES), F32)] * 5
        + [
            pltpu.VMEM((3, steps + 1, UNROLL, LANES), F32),
            pltpu.VMEM((tiles, width, LANES), F32),
            pltpu.VMEM((tiles, width, LANES), F32),
            pltpu.VMEM((tiles, 8, LANES), F32),
            pltpu.VMEM((steps + 3, width, span), BF16),
            pltpu.VMEM((steps + 3, width, span), BF16),
            pltpu.VMEM((steps + 3, width, span), BF16),
            pltpu.VMEM((steps + 3, RADIAL_ROWS, span), BF16),
            pltpu.VMEM((width, span), BF16),
            pltpu.VMEM((width, span), BF16),
            pltpu.VMEM((width, span), F32),
            pltpu.VMEM((width, span), F32),
            pltpu.VMEM((width, span), F32),
            pltpu.VMEM((width, span), F32),
            pltpu.VMEM((width, span), BF16),
            pltpu.VMEM((width, span), BF16),
            pltpu.VMEM((3 * GROUP_ROWS, 128), F32),
        ],
        compiler_params=pltpu.CompilerParams(vmem_limit_bytes=56 * 1024 * 1024),
        cost_estimate=pl.CostEstimate(
            flops=30_000_000_000, bytes_accessed=4_000_000, transcendentals=16_000_000
        ),
    )(
        disp_t,
        index_t,
        neighbour_count,
        species,
        species_scale,
        species_shift,
        features,
        table_t,
        w_f1,
        b_f1,
        w_f2,
        w_o1,
        w_o2,
        w_e1.T,
        b_f2,
        b_o1,
        b_o2,
        b_e1,
        w_e2,
    )
    forces = pl.pallas_call(
        return_kernel,
        out_shape=jax.ShapeDtypeStruct((3, atom_rows), F32),
        in_specs=[vmem] * 6,
        out_specs=vmem,
        scratch_shapes=[
            pltpu.VMEM((ghost_rows // 128, 8, 128), F32),
            pltpu.SemaphoreType.DMA((6,)),
            pltpu.SemaphoreType.DMA((6,)),
        ],
        compiler_params=pltpu.CompilerParams(
            collective_id=1, has_side_effects=True, vmem_limit_bytes=32 * 1024 * 1024
        ),
    )(own_force, spread, *lists, face_counts)
    return (energy, forces)


def solution(mesh):
    both = ("geom", "gx", "gy", "gz")
    return jax.shard_map(
        body,
        mesh=mesh,
        in_specs=(
            P(both, None),
            P(None, both),
            P(both),
            P(both),
            P(both),
            P(both, None, None),
            P(both, None, None),
            P(both, None, None),
            P(both, None),
        )
        + (P(),) * 14,
        out_specs=(P(both), P(None, both)),
        check_vma=False,
    )
```

```python
import math

import jax
import jax.numpy as jnp
from jax import lax
from jax.experimental import pallas as pl
from jax.experimental.pallas import tpu as pltpu
from jax.sharding import PartitionSpec as P

GAMMA = 10.0
CUTOFF = 5.0
LOG_TWO = math.log(2.0)
LOG2E = 1.0 / LOG_TWO
LANES = 128
UNROLL = 4
CHUNK = 256
RADIAL_ROWS = 64
GROUP_ROWS = 32
BEHIND = 2

BF16 = jnp.bfloat16
F32 = jnp.float32


def dot(a, b):
    return jnp.dot(a, b, preferred_element_type=F32)


def dot_nt(a, b):
    return lax.dot_general(a, b, (((1,), (1,)), ((), ())), preferred_element_type=F32)


def split3(value):
    high = value.astype(BF16)
    rest = value - high.astype(F32)
    middle = rest.astype(BF16)
    low = (rest - middle.astype(F32)).astype(BF16)
    return high, middle, low


def split2(value):
    high = value.astype(BF16)
    low = (value - high.astype(F32)).astype(BF16)
    return jnp.concatenate([high, low], axis=0)


def softplus_of(value):
    return jnp.maximum(value, 0.0) + jnp.log(1.0 + jnp.exp(-jnp.abs(value)))


def sigmoid_of(value):
    return 1.0 / (1.0 + jnp.exp(-value))


def one_hot(row, size):
    span = row.shape[1]
    parts = []
    for start in range(0, size, CHUNK):
        spot = jnp.broadcast_to(row - float(start), (16, span)).astype(BF16)
        lanes = lax.broadcasted_iota(jnp.int32, (16, span), 0).astype(F32)
        for b in range(min(CHUNK, size - start) // 16):
            ids = (lanes + float(16 * b)).astype(BF16)
            parts.append(jnp.where(ids == spot, jnp.ones((), BF16), jnp.zeros((), BF16)))
    return jnp.concatenate(parts, axis=0)


def flip(weight):
    return weight.astype(F32).T.astype(BF16)


def pair_kernel(
    rows_ref,
    order_ref,
    counts_ref,
    vals_ref,
    feat_ref,
    table_ref,
    square_ref,
    wide_ref,
    tall_ref,
    column_ref,
    energy_ref,
    own_ref,
    spread_ref,
    msg_ref,
    gm_ref,
    own3_ref,
    xj_ref,
    prod_ref,
    sig_ref,
    slope_ref,
    hid_a_ref,
    hid_b_ref,
    filt_a_ref,
    filt_b_ref,
    found_a_ref,
    found_b_ref,
    back_a_ref,
    back_b_ref,
    minus_a_ref,
    minus_b_ref,
    total_ref,
):
    width, atoms = feat_ref.shape
    tiles = atoms // LANES
    steps = (rows_ref.shape[1] - 1) // tiles
    span = UNROLL * LANES
    table_rows = table_ref.shape[1]
    idle = tiles * steps

    counts = counts_ref[0:1]
    scale = vals_ref[0:1]
    shift = vals_ref[8:9]
    feat = feat_ref[...].astype(F32)
    row_ref, dist_ref, env_ref, near_ref, far_ref = [rows_ref.at[n] for n in range(5)]

    w2, w2t, wo1, wo1t, wo2, wo2t = [square_ref[n] for n in range(6)]
    w1_back, we1 = wide_ref[0], wide_ref[1]
    w1t, we1t = tall_ref[0], tall_ref[1]
    b_f2, b_o1, b_o2, mu, sharp = [column_ref[:, n : n + 1] for n in range(5)]
    mu, sharp = mu[0:RADIAL_ROWS], sharp[0:RADIAL_ROWS]
    b_e1, w_e2 = [column_ref[0 : we1.shape[0], n : n + 1] for n in (5, 6)]

    def lane_row(ref, at):
        return jnp.concatenate([ref[at, u : u + 1, :] for u in range(UNROLL)], axis=1)

    ends = []
    items = jnp.zeros((), jnp.int32)
    for tile in range(tiles):
        most = jnp.max(counts[:, tile * LANES : (tile + 1) * LANES]).astype(jnp.int32)
        items = items + (most + (UNROLL - 1)) // UNROLL
        ends.append(items)
    rounds = (items + 1) // 2
    turns = (items + 3) // 4

    def place(item):
        tile = jnp.zeros((), jnp.int32)
        first = jnp.zeros((), jnp.int32)
        for end in ends[:-1]:
            past = item >= end
            tile = tile + past.astype(jnp.int32)
            first = jnp.where(past, end, first)
        at = jnp.where((item >= 0) & (item < items), tile * steps + item - first, idle)
        return tile, at

    def gather(row):
        return dot(table_ref[...], one_hot(row, table_rows))

    def radial_dot(at):
        offset = lane_row(dist_ref, at) - mu
        basis = jnp.exp2(sharp * (offset * offset))
        return (offset * basis).astype(BF16), dot(w1t, basis.astype(BF16))

    def activate(pre):
        grown = jnp.exp2(pre * LOG2E)
        total = 1.0 + grown
        sig = (grown * pl.reciprocal(total, approx=True)).astype(BF16)
        return sig, (jnp.log2(total) - 1.0).astype(BF16)

    def begin(item, hid_ref):
        slope, pre = radial_dot(place(item)[1])
        slope_ref[item + BEHIND] = slope
        sig, hidden = activate(pre)
        sig_ref[item + BEHIND] = sig
        hid_ref[...] = hidden

    def finish(item, filt_ref, found_ref):
        tile, at = place(item)
        prod = found_ref[...] * filt_ref[...]
        prod_ref[item + BEHIND] = prod.astype(BF16)
        weighted = prod * lane_row(env_ref, at)
        part = msg_ref[tile]
        for u in range(UNROLL):
            part = part + weighted[:, u * LANES : (u + 1) * LANES]
        msg_ref[tile] = part

    def forward(item, hid_ref, next_ref, filt_ref, found_ref, last_filt_ref, last_found_ref):
        filt = dot(w2t, hid_ref[...]) + b_f2
        slope, pre = radial_dot(place(item + 1)[1])
        slope_ref[item + BEHIND + 1] = slope
        found = gather(lane_row(row_ref, place(item)[1]))
        sig, hidden = activate(pre)
        sig_ref[item + BEHIND + 1] = sig
        next_ref[...] = hidden
        finish(item - 1, last_filt_ref, last_found_ref)
        filt_ref[...] = filt
        found_ref[...] = found
        xj_ref[item + BEHIND] = found.astype(BF16)

    msg_ref[...] = jnp.zeros_like(msg_ref)
    filt_b_ref[...] = jnp.zeros_like(filt_b_ref)
    found_b_ref[...] = jnp.zeros_like(found_b_ref)
    begin(jnp.zeros((), jnp.int32), hid_a_ref)

    def forward_round(turn, carry):
        item = 4 * turn
        forward(item, hid_a_ref, hid_b_ref, filt_a_ref, found_a_ref, filt_b_ref, found_b_ref)
        forward(item + 1, hid_b_ref, hid_a_ref, filt_b_ref, found_b_ref, filt_a_ref, found_a_ref)
        forward(item + 2, hid_a_ref, hid_b_ref, filt_a_ref, found_a_ref, filt_b_ref, found_b_ref)
        forward(item + 3, hid_b_ref, hid_a_ref, filt_b_ref, found_b_ref, filt_a_ref, found_a_ref)
        return carry

    lax.fori_loop(0, turns, forward_round, 0)
    finish(4 * turns - 1, filt_b_ref, found_b_ref)

    message = jnp.concatenate([msg_ref[t] for t in range(tiles)], axis=1)
    message = (message * LOG_TWO).astype(BF16)
    out_pre = dot(wo1t, message) + b_o1
    out_mid = (softplus_of(out_pre) - LOG_TWO).astype(BF16)
    updated = (feat + dot(wo2t, out_mid) + b_o2).astype(BF16)
    energy_pre = dot(we1, updated) + b_e1
    soft = softplus_of(energy_pre) - LOG_TWO
    energy = scale * jnp.sum(soft * w_e2, axis=0, keepdims=True) + shift
    home = one_hot(order_ref[0:1], atoms)
    plain = dot(split2(jnp.broadcast_to(energy, (8, atoms))), home)
    energy_ref[...] = (plain[0:1] + plain[8:9]).reshape(atoms)
    grad_head = (scale * w_e2 * sigmoid_of(energy_pre)).astype(BF16)
    grad_update = dot(we1t, grad_head).astype(BF16)
    grad_mid = (dot(wo2, grad_update) * sigmoid_of(out_pre)).astype(BF16)
    grad_message = dot(wo1, grad_mid)
    for tile in range(tiles):
        gm_ref[tile] = grad_message[:, tile * LANES : (tile + 1) * LANES]

    total_ref[...] = jnp.zeros_like(total_ref)
    own3_ref[...] = jnp.zeros_like(own3_ref)
    for ref in (back_a_ref, back_b_ref, minus_a_ref, minus_b_ref):
        ref[...] = jnp.zeros_like(ref)
    for early in range(BEHIND):
        prod_ref[early] = jnp.zeros((width, span), BF16)
        slope_ref[early] = jnp.zeros((RADIAL_ROWS, span), BF16)
    for late in range(4):
        ahead = 2 * rounds + BEHIND + late
        xj_ref[ahead] = jnp.zeros((width, span), BF16)
        prod_ref[ahead] = jnp.zeros((width, span), BF16)
        slope_ref[ahead] = jnp.zeros((RADIAL_ROWS, span), BF16)
        sig_ref[ahead] = jnp.zeros((width, span), BF16)

    def pull(item):
        tile, at = place(item)
        grad_b = gm_ref[tile].astype(BF16)
        grad_b_wide = jnp.concatenate([grad_b] * UNROLL, axis=1)
        mixed = dot(w2, grad_b_wide * xj_ref[item + BEHIND])
        return (mixed * sig_ref[item + BEHIND].astype(F32)).astype(BF16)

    def settle(item, grad_pre):
        tile, at = place(item)
        grad_basis = dot(w1_back, grad_pre)
        grad_wide = jnp.concatenate([gm_ref[tile]] * UNROLL, axis=1)
        s1 = jnp.sum(grad_basis * slope_ref[item + BEHIND].astype(F32), axis=0, keepdims=True)
        s2 = jnp.sum(grad_wide * prod_ref[item + BEHIND].astype(F32), axis=0, keepdims=True)
        ratio = s1 * lane_row(near_ref, at) + s2 * lane_row(far_ref, at)
        forces = []
        for c in range(3):
            force = ratio * lane_row(rows_ref.at[5 + c], at)
            part = own3_ref[tile, c : c + 1, :]
            for u in range(UNROLL):
                part = part + force[:, u * LANES : (u + 1) * LANES]
            own3_ref[tile, c : c + 1, :] = part
            forces.append(-force)
        return jnp.concatenate(forces, axis=0)

    def strew(item, minus):
        row = lane_row(row_ref, place(item)[1])
        high = jnp.floor(row * (1.0 / 128))
        low = row - high * 128.0
        wide = (16, span)
        high_b = jnp.broadcast_to(high, wide).astype(BF16)
        low_b = jnp.broadcast_to(low, wide).astype(BF16)
        lanes = lax.broadcasted_iota(jnp.int32, wide, 0).astype(F32)
        ids = [(lanes + float(16 * b)).astype(BF16) for b in range(8)]
        lower = jnp.concatenate(
            [jnp.where(one == low_b, jnp.ones((), BF16), jnp.zeros((), BF16)) for one in ids],
            axis=0,
        )
        here = [ids[b] == high_b for b in range(GROUP_ROWS // 16)]
        placed = []
        for c in range(3):
            part = jnp.broadcast_to(minus[c : c + 1], wide).astype(BF16)
            placed += [jnp.where(mask, part, jnp.zeros((), BF16)) for mask in here]
        return dot_nt(jnp.concatenate(placed, axis=0), lower)

    def backward_round(turn, carry):
        item = 2 * turn
        spread_a = strew(item - 4, minus_a_ref[0:3])
        spread_b = strew(item - 3, minus_b_ref[0:3])
        minus_a = settle(item - 2, back_a_ref[...])
        minus_b = settle(item - 1, back_b_ref[...])
        pull_a = pull(item)
        pull_b = pull(item + 1)
        total_ref[...] = total_ref[...] + spread_a + spread_b
        minus_a_ref[0:3] = minus_a
        minus_b_ref[0:3] = minus_b
        back_a_ref[...] = pull_a
        back_b_ref[...] = pull_b
        return carry

    lax.fori_loop(0, rounds + 2, backward_round, 0)

    for tile in range(tiles):
        own_ref[:, tile * LANES : (tile + 1) * LANES] = own3_ref[tile]
    spread_ref[...] = jnp.zeros_like(spread_ref)
    for c in range(3):
        spread_ref[:, c, :] = total_ref[c * GROUP_ROWS : c * GROUP_ROWS + spread_ref.shape[0]]


def neighbours():
    found = []
    for axis in ("gx", "gy", "gz"):
        size = lax.axis_size(axis)
        place = lax.axis_index(axis)
        found.append({axis: lax.rem(place + 1, size)})
        found.append({axis: lax.rem(place + size - 1, size)})
    return found


def greet(found):
    barrier = pltpu.get_barrier_semaphore()
    for device in found:
        pl.semaphore_signal(
            barrier, inc=1, device_id=device, device_id_type=pl.DeviceIdType.MESH
        )
    pl.semaphore_wait(barrier, len(found))


FACES = ((0, 1, 1, 0), (0, 0, 0, 1), (1, 1, 3, 2), (1, 0, 2, 3), (2, 1, 5, 4), (2, 0, 4, 5))


def ready_weights(
    w1_ref,
    b1_ref,
    w2_ref,
    wo1_ref,
    wo2_ref,
    we1_ref,
    bf2_ref,
    bo1_ref,
    bo2_ref,
    be1_ref,
    w_e2_ref,
    square_ref,
    wide_ref,
    tall_ref,
    column_ref,
):
    radial, width = w1_ref.shape
    bias = b1_ref[...].reshape(1, width)
    bias_high = bias.astype(BF16).astype(F32)
    bias_middle = (bias - bias_high).astype(BF16).astype(F32)
    w1 = jnp.concatenate(
        [
            w1_ref[...].astype(F32),
            bias_high,
            bias_middle,
            bias - bias_high - bias_middle,
            jnp.zeros((RADIAL_ROWS - radial - 3, width), F32),
        ],
        axis=0,
    )
    radial_col = lax.broadcasted_iota(jnp.int32, (RADIAL_ROWS, 1), 0)
    tall_ref[0] = w1.T.astype(BF16)
    wide_ref[0] = jnp.where(radial_col < radial, w1, 0.0).astype(BF16)
    wide_ref[1] = we1_ref[...]
    tall_ref[1] = flip(we1_ref[...])
    for n, ref in enumerate((w2_ref, wo1_ref, wo2_ref)):
        square_ref[2 * n] = ref[...]
        square_ref[2 * n + 1] = flip(ref[...])
    ids = lax.broadcasted_iota(jnp.int32, (1, width), 1)
    rows = [
        bf2_ref[...].reshape(1, width) * LOG2E,
        bo1_ref[...].reshape(1, width),
        bo2_ref[...].reshape(1, width),
        ids.astype(F32) * (CUTOFF / (radial - 1)),
        jnp.where(ids < radial, -GAMMA * LOG2E, 0.0),
    ]
    for ref in (be1_ref, w_e2_ref):
        size = ref.shape[0]
        rows.append(
            jnp.concatenate(
                [ref[...].reshape(1, size), jnp.zeros((1, width - size), F32)], axis=1
            )
        )
    rows.append(jnp.zeros((width - len(rows), width), F32))
    column_ref[...] = jnp.concatenate(rows, axis=0).T


def prepare(
    feat_ref,
    disp_ref,
    index_ref,
    count_ref,
    species_ref,
    scale_ref,
    shift_ref,
    rows_ref,
    order_ref,
    counts_ref,
    vals_ref,
    sorted_ref,
    raw_ref,
    rank_ref,
):
    atoms = feat_ref.shape[0]
    slots = disp_ref.shape[1] // atoms
    tiles = atoms // LANES
    steps = slots // UNROLL
    idle = tiles * steps
    block = math.lcm(slots, LANES)
    lines = block // LANES
    each = block // slots
    groups = atoms // each

    raw_ref[...] = jnp.zeros_like(raw_ref)

    def lay(g, carry):
        for m in range(lines):
            at = pl.multiple_of((g * lines + m) * LANES, LANES)
            three = disp_ref[:, pl.ds(at, LANES)]
            for c in range(3):
                raw_ref[c, m, pl.ds(g, 1), :] = three[c : c + 1]
            line = index_ref[pl.ds(g * lines + m, 1), :]
            raw_ref[3, m, pl.ds(g, 1), :] = line.astype(F32)
        return carry

    lax.fori_loop(0, groups, lay, 0)

    atom_row = lax.broadcasted_iota(jnp.int32, (1, atoms), 1)
    atom_col = lax.broadcasted_iota(jnp.int32, (atoms, 1), 0)
    count_row = count_ref[...].reshape(1, atoms)
    key_row = (count_row * atoms - atom_row).astype(F32)
    count_col = jnp.broadcast_to(count_row.astype(F32), (128, atoms)).T[:, 0:1]
    key_col = count_col * float(atoms) - atom_col.astype(F32)
    rank_col = jnp.sum(jnp.where(key_row > key_col, 1.0, 0.0), axis=1, keepdims=True)
    perm = jnp.where(rank_col == atom_row.astype(F32), 1.0, 0.0).astype(BF16)

    rank_ref[...] = jnp.broadcast_to(rank_col, (atoms, LANES))
    order_ref[...] = rank_ref[...].T[0:8]
    lane_ids = lax.broadcasted_iota(jnp.int32, (groups, LANES), 1).astype(F32)
    blocks = []
    for a in range(each):
        rank = rank_ref[pl.ds(a, groups, stride=each), :]
        blocks.append(
            jnp.concatenate(
                [
                    jnp.where(rank - float(t * LANES) == lane_ids, 1.0, 0.0).astype(BF16)
                    for t in range(tiles)
                ],
                axis=1,
            )
        )
        if groups < LANES:
            blocks.append(jnp.zeros((LANES - groups, atoms), BF16))
    spots = jnp.concatenate(blocks, axis=0)

    def columns(c):
        turned = jnp.concatenate([raw_ref[c, m].T for m in range(lines)], axis=0)
        return jnp.concatenate(
            [turned[a * slots : (a + 1) * slots] for a in range(each)], axis=1
        )

    def put(ref, value):
        for tile in range(tiles):
            for s in range(steps):
                ref[tile * steps + s] = value[
                    s * UNROLL : (s + 1) * UNROLL, tile * LANES : (tile + 1) * LANES
                ]
        ref[idle] = jnp.zeros((UNROLL, LANES), F32)

    raw = jnp.concatenate([columns(c) for c in range(3)], axis=0)
    index = columns(3)
    index_high = jnp.floor(index * (1.0 / 128))
    index_low = index - index_high * 128.0
    stack = jnp.concatenate(
        list(split3(raw)) + [index_high.astype(BF16), index_low.astype(BF16)], axis=0
    )
    found = dot(stack, spots)
    size = 3 * slots
    disp = found[0:size] + found[size : 2 * size] + found[2 * size : 3 * size]
    put(
        rows_ref.at[0],
        found[3 * size : 3 * size + slots] * 128.0 + found[3 * size + slots : 3 * size + 2 * slots],
    )
    counts8 = dot(jnp.broadcast_to(count_row, (8, atoms)).astype(F32).astype(BF16), perm)
    counts = counts8[0:1]
    counts_ref[...] = counts8
    kinds = scale_ref.shape[0]
    kind_ids = lax.broadcasted_iota(jnp.int32, (kinds, 1), 0)
    kind_pick = jnp.where(kind_ids == species_ref[...].reshape(1, atoms), 1.0, 0.0).astype(BF16)
    pair_of = jnp.concatenate(
        [
            jnp.broadcast_to(scale_ref[...].reshape(1, kinds), (8, kinds)),
            jnp.broadcast_to(shift_ref[...].reshape(1, kinds), (8, kinds)),
        ],
        axis=0,
    )
    atom_vals = sum(dot(part, kind_pick) for part in split3(pair_of))
    vals_ref[...] = sum(dot(part, perm) for part in split3(atom_vals))
    sorted_ref[...] = dot(feat_ref[...].astype(F32).T.astype(BF16), perm).astype(BF16)

    dx = disp[0:slots]
    dy = disp[slots : 2 * slots]
    dz = disp[2 * slots : 3 * slots]
    squared = dx * dx + dy * dy + dz * dz
    distance = jnp.sqrt(squared)
    put(rows_ref.at[1], distance)
    slot_ids = lax.broadcasted_iota(jnp.int32, (slots, 1), 0).astype(F32)
    live = jnp.where(slot_ids < counts, 1.0, 0.0)
    y = (math.pi / CUTOFF) * distance - 0.5 * math.pi
    y2 = y * y
    sin_y = y * (
        1.0
        + y2
        * (
            -1.0 / 6
            + y2 * (1.0 / 120 + y2 * (-1.0 / 5040 + y2 * (1.0 / 362880 - y2 * (1.0 / 39916800))))
        )
    )
    envelope = (0.5 - 0.5 * sin_y) * live
    put(rows_ref.at[2], envelope)
    cos_y = 1.0 + y2 * (
        -0.5
        + y2
        * (
            1.0 / 24
            + y2
            * (
                -1.0 / 720
                + y2 * (1.0 / 40320 + y2 * (-1.0 / 3628800 + y2 * (1.0 / 479001600)))
            )
        )
    )
    inverse = live / distance
    put(rows_ref.at[3], envelope * (-2.0 * GAMMA) * inverse)
    put(rows_ref.at[4], (-0.5 * math.pi / CUTOFF * LOG_TWO) * cos_y * inverse)
    put(rows_ref.at[5], dx)
    put(rows_ref.at[6], dy)
    put(rows_ref.at[7], dz)


INPUTS = 23
OUTPUTS = 9


def named_faces(lists, used_ref):
    found = []
    used = used_ref[...]
    for dim, side, column, _ in FACES:
        names = lists[dim][side : side + 1, :]
        lanes = lax.broadcasted_iota(jnp.int32, names.shape, 1)
        found.append(jnp.where(lanes < used[:, column : column + 1], names, -1).astype(F32))
    return found


def send_kernel(*refs):
    far, refs = refs[:INPUTS], refs[INPUTS:]
    table_ref, results, refs = refs[0], refs[1 : OUTPUTS + 1], refs[OUTPUTS + 1 :]
    near, made, refs = refs[:INPUTS], refs[INPUTS : INPUTS + OUTPUTS], refs[INPUTS + OUTPUTS :]
    mine_ref, stage_ref, raw_ref, rank_ref, load_sem, save_sem, send_sem, recv_sem = refs
    loads = [
        pltpu.make_async_copy(one, two, load_sem.at[n])
        for n, (one, two) in enumerate(zip(far, near))
    ]
    for load in loads:
        load.start()
    found = neighbours()
    greet(found)
    feat_ref, w_ref = near[0:2]
    atoms = feat_ref.shape[0]
    for load in loads[0:6]:
        load.wait()
    x_t = dot(feat_ref[...], w_ref[...]).T.astype(BF16)
    copies = []
    start = 0
    for n, names in enumerate(named_faces(near[2:5], near[5])):
        length = names.shape[1]
        stage_ref[:, start : start + length] = dot(x_t, one_hot(names, atoms)).astype(BF16)
        copy = pltpu.make_async_remote_copy(
            src_ref=stage_ref.at[:, pl.ds(start, length)],
            dst_ref=table_ref.at[:, pl.ds(atoms + start, length)],
            send_sem=send_sem.at[n],
            recv_sem=recv_sem.at[n],
            device_id=found[n],
            device_id_type=pl.DeviceIdType.MESH,
        )
        copy.start()
        copies.append(copy)
        start += length
    mine_ref[...] = x_t
    saves = [pltpu.make_async_copy(mine_ref, table_ref.at[:, pl.ds(0, atoms)], save_sem.at[0])]
    saves[0].start()
    for load in loads[6:]:
        load.wait()
    rows_ref, order_ref, counts_ref, vals_ref, sorted_ref = made[0:5]
    prepare(
        feat_ref,
        *near[6:12],
        rows_ref,
        order_ref,
        counts_ref,
        vals_ref,
        sorted_ref,
        raw_ref,
        rank_ref,
    )
    ready_weights(*near[12:], *made[5:])
    for n, (one, two) in enumerate(zip(made, results)):
        save = pltpu.make_async_copy(one, two, save_sem.at[n + 1])
        save.start()
        saves.append(save)
    for copy in saves + copies:
        copy.wait()


def return_kernel(
    own_ref,
    spread_ref,
    order_ref,
    ex_ref,
    ey_ref,
    ez_ref,
    used_ref,
    force_ref,
    own_here,
    order_here,
    ex_here,
    ey_here,
    ez_here,
    used_here,
    mine_ref,
    land_ref,
    load_sem,
    send_sem,
    recv_sem,
):
    atoms = force_ref.shape[1]
    group = atoms // 128
    pairs = (
        (spread_ref.at[pl.ds(0, group)], mine_ref),
        (own_ref, own_here),
        (order_ref, order_here),
        (ex_ref, ex_here),
        (ey_ref, ey_here),
        (ez_ref, ez_here),
        (used_ref, used_here),
    )
    loads = [
        pltpu.make_async_copy(one, two, load_sem.at[n]) for n, (one, two) in enumerate(pairs)
    ]
    for load in loads:
        load.start()
    lists = (ex_here, ey_here, ez_here)
    found = neighbours()
    greet(found)
    copies = []
    start = 0
    for n, (dim, _, _, to) in enumerate(FACES):
        length = lists[dim].shape[1] // 128
        copy = pltpu.make_async_remote_copy(
            src_ref=spread_ref.at[pl.ds(group + start, length)],
            dst_ref=land_ref.at[pl.ds(start, length)],
            send_sem=send_sem.at[n],
            recv_sem=recv_sem.at[n],
            device_id=found[to ^ 1],
            device_id_type=pl.DeviceIdType.MESH,
        )
        copy.start()
        copies.append(copy)
        start += length
    for load in loads:
        load.wait()
    picks = jnp.concatenate(
        [one_hot(names, atoms) for names in named_faces(lists, used_here)], axis=1
    )
    total = jnp.concatenate([mine_ref[h] for h in range(group)], axis=1)
    part = dot(split2(own_here[...]), one_hot(order_here[0:1], atoms))
    total = total + part[0:8] + part[8:16]
    for copy in copies:
        copy.wait()
    values = jnp.concatenate([land_ref[h] for h in range(start)], axis=1)
    part = dot_nt(split2(values), picks)
    total = total + part[0:8] + part[8:16]
    force_ref[...] = total[0:3]


def body(
    features,
    displacement,
    neighbour,
    neighbour_count,
    species,
    exports_x,
    exports_y,
    exports_z,
    face_counts,
    w_in,
    w_f1,
    b_f1,
    w_f2,
    b_f2,
    w_o1,
    b_o1,
    w_o2,
    b_o2,
    w_e1,
    b_e1,
    w_e2,
    species_scale,
    species_shift,
):
    atom_rows, width = features.shape
    slot_count = neighbour.shape[0] // atom_rows
    vmem = pl.BlockSpec(memory_space=pltpu.VMEM)
    lists = (exports_x[0], exports_y[0], exports_z[0])
    ghost_rows = sum(2 * one.shape[1] for one in lists)
    table_rows = atom_rows + ghost_rows
    tiles = atom_rows // LANES
    steps = slot_count // UNROLL * tiles
    groups = table_rows // 128
    lines = math.lcm(slot_count, LANES) // LANES
    inputs = (
        features,
        w_in,
        *lists,
        face_counts,
        displacement,
        neighbour.reshape(-1, LANES),
        neighbour_count,
        species,
        species_scale,
        species_shift,
        w_f1,
        b_f1,
        w_f2,
        w_o1,
        w_o2,
        w_e1.T,
        b_f2,
        b_o1,
        b_o2,
        b_e1,
        w_e2,
    )
    hidden = w_e1.shape[1]
    anywhere = pl.BlockSpec(memory_space=pl.ANY)
    results = (
        jax.ShapeDtypeStruct((8, steps + 1, UNROLL, LANES), F32),
        jax.ShapeDtypeStruct((8, atom_rows), F32),
        jax.ShapeDtypeStruct((8, atom_rows), F32),
        jax.ShapeDtypeStruct((16, atom_rows), F32),
        jax.ShapeDtypeStruct((width, atom_rows), BF16),
        jax.ShapeDtypeStruct((6, width, width), BF16),
        jax.ShapeDtypeStruct((2, hidden, width), BF16),
        jax.ShapeDtypeStruct((2, width, hidden), BF16),
        jax.ShapeDtypeStruct((width, width), F32),
    )
    table_t, rows, order, counts, vals, sorted_t, *weights = pl.pallas_call(
        send_kernel,
        out_shape=(jax.ShapeDtypeStruct((width, table_rows), BF16),) + results,
        in_specs=[anywhere] * len(inputs),
        out_specs=(anywhere,) * (1 + len(results)),
        scratch_shapes=[pltpu.VMEM(one.shape, one.dtype) for one in inputs + results]
        + [
            pltpu.VMEM((width, atom_rows), BF16),
            pltpu.VMEM((width, ghost_rows), BF16),
            pltpu.VMEM((4, lines, LANES, LANES), F32),
            pltpu.VMEM((atom_rows, LANES), F32),
            pltpu.SemaphoreType.DMA((len(inputs),)),
            pltpu.SemaphoreType.DMA((1 + len(results),)),
            pltpu.SemaphoreType.DMA((6,)),
            pltpu.SemaphoreType.DMA((6,)),
        ],
        compiler_params=pltpu.CompilerParams(
            collective_id=0, has_side_effects=True, vmem_limit_bytes=58 * 1024 * 1024
        ),
    )(*inputs)
    span = UNROLL * LANES
    energy, own_force, spread = pl.pallas_call(
        pair_kernel,
        out_shape=(
            jax.ShapeDtypeStruct((atom_rows,), F32),
            jax.ShapeDtypeStruct((8, atom_rows), F32),
            jax.ShapeDtypeStruct((groups, 8, 128), F32),
        ),
        in_specs=[vmem] * 10,
        out_specs=(vmem, vmem, vmem),
        scratch_shapes=[
            pltpu.VMEM((tiles, width, LANES), F32),
            pltpu.VMEM((tiles, width, LANES), F32),
            pltpu.VMEM((tiles, 8, LANES), F32),
            pltpu.VMEM((steps + 10, width, span), BF16),
            pltpu.VMEM((steps + 10, width, span), BF16),
            pltpu.VMEM((steps + 10, width, span), BF16),
            pltpu.VMEM((steps + 10, RADIAL_ROWS, span), BF16),
            pltpu.VMEM((width, span), BF16),
            pltpu.VMEM((width, span), BF16),
            pltpu.VMEM((width, span), F32),
            pltpu.VMEM((width, span), F32),
            pltpu.VMEM((width, span), F32),
            pltpu.VMEM((width, span), F32),
            pltpu.VMEM((width, span), BF16),
            pltpu.VMEM((width, span), BF16),
            pltpu.VMEM((8, span), F32),
            pltpu.VMEM((8, span), F32),
            pltpu.VMEM((3 * GROUP_ROWS, 128), F32),
        ],
        compiler_params=pltpu.CompilerParams(vmem_limit_bytes=58 * 1024 * 1024),
        cost_estimate=pl.CostEstimate(
            flops=30_000_000_000, bytes_accessed=4_000_000, transcendentals=16_000_000
        ),
    )(
        rows,
        order,
        counts,
        vals,
        sorted_t,
        table_t,
        *weights,
    )
    last = (own_force, spread, order, *lists, face_counts)
    copied = (own_force, order, *lists, face_counts)
    forces = pl.pallas_call(
        return_kernel,
        out_shape=jax.ShapeDtypeStruct((3, atom_rows), F32),
        in_specs=[anywhere] * len(last),
        out_specs=vmem,
        scratch_shapes=[pltpu.VMEM(one.shape, one.dtype) for one in copied]
        + [
            pltpu.VMEM((tiles, 8, LANES), F32),
            pltpu.VMEM((ghost_rows // 128, 8, 128), F32),
            pltpu.SemaphoreType.DMA((len(last),)),
            pltpu.SemaphoreType.DMA((6,)),
            pltpu.SemaphoreType.DMA((6,)),
        ],
        compiler_params=pltpu.CompilerParams(
            collective_id=1, has_side_effects=True, vmem_limit_bytes=58 * 1024 * 1024
        ),
    )(*last)
    return (energy, forces)


def solution(mesh):
    both = ("geom", "gx", "gy", "gz")
    return jax.shard_map(
        body,
        mesh=mesh,
        in_specs=(
            P(both, None),
            P(None, both),
            P(both),
            P(both),
            P(both),
            P(both, None, None),
            P(both, None, None),
            P(both, None, None),
            P(both, None),
        )
        + (P(),) * 14,
        out_specs=(P(both), P(None, both)),
        check_vma=False,
    )
```

```python
import functools
import math

import jax
import jax.numpy as jnp
from jax import lax
from jax.experimental import pallas as pl
from jax.experimental.pallas import tpu as pltpu
from jax.sharding import PartitionSpec as P

GAMMA = 10.0
CUTOFF = 5.0
LOG_TWO = math.log(2.0)
LOG2E = 1.0 / LOG_TWO
LANES = 128
UNROLL = 4
CHUNK = 256
RADIAL_ROWS = 64
GROUP_ROWS = 32
BEHIND = 2

BF16 = jnp.bfloat16
F32 = jnp.float32


def dot(a, b):
    return jnp.dot(a, b, preferred_element_type=F32)


def dot_nt(a, b):
    return lax.dot_general(a, b, (((1,), (1,)), ((), ())), preferred_element_type=F32)


def split3(value):
    high = value.astype(BF16)
    rest = value - high.astype(F32)
    middle = rest.astype(BF16)
    low = (rest - middle.astype(F32)).astype(BF16)
    return high, middle, low


def split2(value):
    high = value.astype(BF16)
    low = (value - high.astype(F32)).astype(BF16)
    return jnp.concatenate([high, low], axis=0)


def softplus_of(value):
    return jnp.maximum(value, 0.0) + jnp.log(1.0 + jnp.exp(-jnp.abs(value)))


def sigmoid_of(value):
    return 1.0 / (1.0 + jnp.exp(-value))


def one_hot(row, size):
    span = row.shape[1]
    parts = []
    for start in range(0, size, CHUNK):
        spot = jnp.broadcast_to(row - float(start), (16, span)).astype(BF16)
        lanes = lax.broadcasted_iota(jnp.int32, (16, span), 0).astype(F32)
        for b in range(min(CHUNK, size - start) // 16):
            ids = (lanes + float(16 * b)).astype(BF16)
            parts.append(jnp.where(ids == spot, jnp.ones((), BF16), jnp.zeros((), BF16)))
    return jnp.concatenate(parts, axis=0)


def flip(weight):
    return weight.astype(F32).T.astype(BF16)


def pair_kernel(
    lengths,
    rows_ref,
    order_ref,
    counts_ref,
    vals_ref,
    feat_ref,
    table_ref,
    square_ref,
    wide_ref,
    tall_ref,
    column_ref,
    held_ref,
    energy_ref,
    own_ref,
    spread_ref,
    msg_ref,
    gm_ref,
    own3_ref,
    xj_ref,
    prod_ref,
    sig_ref,
    slope_ref,
    hid_a_ref,
    hid_b_ref,
    filt_a_ref,
    filt_b_ref,
    found_a_ref,
    found_b_ref,
    back_a_ref,
    back_b_ref,
    minus_a_ref,
    minus_b_ref,
    total_ref,
    packed_ref,
):
    width, atoms = feat_ref.shape
    tiles = atoms // LANES
    steps = (rows_ref.shape[1] - 1) // tiles
    span = UNROLL * LANES
    table_rows = table_ref.shape[1]
    idle = tiles * steps

    counts = counts_ref[0:1]
    scale = vals_ref[0:1]
    shift = vals_ref[8:9]
    feat = feat_ref[...].astype(F32)
    row_ref, dist_ref, env_ref, near_ref, far_ref = [rows_ref.at[n] for n in range(5)]

    w2, w2t, wo1, wo1t, wo2, wo2t = [square_ref[n] for n in range(6)]
    w1_back, we1 = wide_ref[0], wide_ref[1]
    w1t, we1t = tall_ref[0], tall_ref[1]
    b_f2, b_o1, b_o2, mu, sharp = [column_ref[:, n : n + 1] for n in range(5)]
    mu, sharp = mu[0:RADIAL_ROWS], sharp[0:RADIAL_ROWS]
    b_e1, w_e2 = [column_ref[0 : we1.shape[0], n : n + 1] for n in (5, 6)]

    def lane_row(ref, at):
        return jnp.concatenate([ref[at, u : u + 1, :] for u in range(UNROLL)], axis=1)

    ends = []
    items = jnp.zeros((), jnp.int32)
    for tile in range(tiles):
        most = jnp.max(counts[:, tile * LANES : (tile + 1) * LANES]).astype(jnp.int32)
        items = items + (most + (UNROLL - 1)) // UNROLL
        ends.append(items)
    rounds = (items + 1) // 2
    turns = (items + 3) // 4

    def place(item):
        tile = jnp.zeros((), jnp.int32)
        first = jnp.zeros((), jnp.int32)
        for end in ends[:-1]:
            past = item >= end
            tile = tile + past.astype(jnp.int32)
            first = jnp.where(past, end, first)
        at = jnp.where((item >= 0) & (item < items), tile * steps + item - first, idle)
        return tile, at

    packed_ref[...] = jnp.zeros_like(packed_ref)
    packed_ref[:, 0:atoms] = table_ref[:, 0:atoms]
    lane_ids = lax.broadcasted_iota(jnp.int32, (width, LANES), 1)
    packed_rows = jnp.full((), atoms, jnp.int32)
    edge = atoms
    for n, length in enumerate(lengths):
        turn = packed_rows & (LANES - 1)
        base = packed_rows - turn
        below = lane_ids < turn
        first = pl.multiple_of(base, LANES)
        last = packed_ref[:, pl.ds(first, LANES)].astype(F32)
        for t in range(length // LANES):
            slab = table_ref[:, edge + t * LANES : edge + (t + 1) * LANES].astype(F32)
            slab = pltpu.roll(slab, turn, 1)
            at = pl.multiple_of(base + t * LANES, LANES)
            packed_ref[:, pl.ds(at, LANES)] = jnp.where(below, last, slab).astype(BF16)
            last = slab
        at = pl.multiple_of(base + length, LANES)
        packed_ref[:, pl.ds(at, LANES)] = jnp.where(below, last, 0.0).astype(BF16)
        packed_rows = packed_rows + held_ref[n, 0]
        edge += length

    def radial_dot(at):
        offset = lane_row(dist_ref, at) - mu
        basis = jnp.exp2(sharp * (offset * offset))
        return (offset * basis).astype(BF16), dot(w1t, basis.astype(BF16))

    def activate(pre):
        grown = jnp.exp2(pre * LOG2E)
        total = 1.0 + grown
        sig = (grown * pl.reciprocal(total, approx=True)).astype(BF16)
        return sig, (jnp.log2(total) - 1.0).astype(BF16)

    def begin(item, hid_ref):
        slope, pre = radial_dot(place(item)[1])
        slope_ref[item + BEHIND] = slope
        sig, hidden = activate(pre)
        sig_ref[item + BEHIND] = sig
        hid_ref[...] = hidden

    def finish(item, filt_ref, found_ref):
        tile, at = place(item)
        prod = found_ref[...] * filt_ref[...]
        prod_ref[item + BEHIND] = prod.astype(BF16)
        weighted = prod * lane_row(env_ref, at)
        part = msg_ref[tile]
        for u in range(UNROLL):
            part = part + weighted[:, u * LANES : (u + 1) * LANES]
        msg_ref[tile] = part

    def forward(size, item, hid_ref, next_ref, filt_ref, found_ref, last_filt_ref, last_found_ref):
        filt = dot(w2t, hid_ref[...]) + b_f2
        slope, pre = radial_dot(place(item + 1)[1])
        slope_ref[item + BEHIND + 1] = slope
        picked = one_hot(lane_row(rows_ref.at[8], place(item)[1]), size)
        found = dot(packed_ref[:, 0:size], picked)
        sig, hidden = activate(pre)
        sig_ref[item + BEHIND + 1] = sig
        next_ref[...] = hidden
        finish(item - 1, last_filt_ref, last_found_ref)
        filt_ref[...] = filt
        found_ref[...] = found
        xj_ref[item + BEHIND] = found.astype(BF16)

    msg_ref[...] = jnp.zeros_like(msg_ref)
    filt_b_ref[...] = jnp.zeros_like(filt_b_ref)
    found_b_ref[...] = jnp.zeros_like(found_b_ref)
    begin(jnp.zeros((), jnp.int32), hid_a_ref)

    def forward_all(size):
        def forward_round(turn, carry):
            a = (filt_a_ref, found_a_ref)
            b = (filt_b_ref, found_b_ref)
            for n in range(0, 4, 2):
                item = 4 * turn + n
                forward(size, item, hid_a_ref, hid_b_ref, *a, *b)
                forward(size, item + 1, hid_b_ref, hid_a_ref, *b, *a)
            return carry

        lax.fori_loop(0, turns, forward_round, 0)

    most = -(-table_rows // CHUNK) * CHUNK
    sizes = [size for size in range(most - 3 * CHUNK, most + 1, CHUNK) if size > 0]
    for n, size in enumerate(sizes):
        fits = packed_rows <= size
        if n:
            fits = fits & (packed_rows > sizes[n - 1])

        @pl.when(fits)
        def _(size=size):
            forward_all(size)

    finish(4 * turns - 1, filt_b_ref, found_b_ref)

    message = jnp.concatenate([msg_ref[t] for t in range(tiles)], axis=1)
    message = (message * LOG_TWO).astype(BF16)
    out_pre = dot(wo1t, message) + b_o1
    out_mid = (softplus_of(out_pre) - LOG_TWO).astype(BF16)
    updated = (feat + dot(wo2t, out_mid) + b_o2).astype(BF16)
    energy_pre = dot(we1, updated) + b_e1
    soft = softplus_of(energy_pre) - LOG_TWO
    energy = scale * jnp.sum(soft * w_e2, axis=0, keepdims=True) + shift
    home = one_hot(order_ref[0:1], atoms)
    plain = dot(split2(jnp.broadcast_to(energy, (8, atoms))), home)
    energy_ref[...] = (plain[0:1] + plain[8:9]).reshape(atoms)
    grad_head = (scale * w_e2 * sigmoid_of(energy_pre)).astype(BF16)
    grad_update = dot(we1t, grad_head).astype(BF16)
    grad_mid = (dot(wo2, grad_update) * sigmoid_of(out_pre)).astype(BF16)
    grad_message = dot(wo1, grad_mid)
    for tile in range(tiles):
        gm_ref[tile] = grad_message[:, tile * LANES : (tile + 1) * LANES]

    total_ref[...] = jnp.zeros_like(total_ref)
    own3_ref[...] = jnp.zeros_like(own3_ref)
    for ref in (back_a_ref, back_b_ref, minus_a_ref, minus_b_ref):
        ref[...] = jnp.zeros_like(ref)
    for early in range(BEHIND):
        prod_ref[early] = jnp.zeros((width, span), BF16)
        slope_ref[early] = jnp.zeros((RADIAL_ROWS, span), BF16)
    for late in range(4):
        ahead = 2 * rounds + BEHIND + late
        xj_ref[ahead] = jnp.zeros((width, span), BF16)
        prod_ref[ahead] = jnp.zeros((width, span), BF16)
        slope_ref[ahead] = jnp.zeros((RADIAL_ROWS, span), BF16)
        sig_ref[ahead] = jnp.zeros((width, span), BF16)

    def pull(item):
        tile, at = place(item)
        grad_b = gm_ref[tile].astype(BF16)
        grad_b_wide = jnp.concatenate([grad_b] * UNROLL, axis=1)
        mixed = dot(w2, grad_b_wide * xj_ref[item + BEHIND])
        return (mixed * sig_ref[item + BEHIND].astype(F32)).astype(BF16)

    def settle(item, grad_pre):
        tile, at = place(item)
        grad_basis = dot(w1_back, grad_pre)
        grad_wide = jnp.concatenate([gm_ref[tile]] * UNROLL, axis=1)
        s1 = jnp.sum(grad_basis * slope_ref[item + BEHIND].astype(F32), axis=0, keepdims=True)
        s2 = jnp.sum(grad_wide * prod_ref[item + BEHIND].astype(F32), axis=0, keepdims=True)
        ratio = s1 * lane_row(near_ref, at) + s2 * lane_row(far_ref, at)
        forces = []
        for c in range(3):
            force = ratio * lane_row(rows_ref.at[5 + c], at)
            part = own3_ref[tile, c : c + 1, :]
            for u in range(UNROLL):
                part = part + force[:, u * LANES : (u + 1) * LANES]
            own3_ref[tile, c : c + 1, :] = part
            forces.append(-force)
        return jnp.concatenate(forces, axis=0)

    def strew(item, minus):
        row = lane_row(row_ref, place(item)[1])
        high = jnp.floor(row * (1.0 / 128))
        low = row - high * 128.0
        wide = (16, span)
        high_b = jnp.broadcast_to(high, wide).astype(BF16)
        low_b = jnp.broadcast_to(low, wide).astype(BF16)
        lanes = lax.broadcasted_iota(jnp.int32, wide, 0).astype(F32)
        ids = [(lanes + float(16 * b)).astype(BF16) for b in range(8)]
        lower = jnp.concatenate(
            [jnp.where(one == low_b, jnp.ones((), BF16), jnp.zeros((), BF16)) for one in ids],
            axis=0,
        )
        here = [ids[b] == high_b for b in range(GROUP_ROWS // 16)]
        placed = []
        for c in range(3):
            part = jnp.broadcast_to(minus[c : c + 1], wide).astype(BF16)
            placed += [jnp.where(mask, part, jnp.zeros((), BF16)) for mask in here]
        return dot_nt(jnp.concatenate(placed, axis=0), lower)

    def backward_round(turn, carry):
        item = 2 * turn
        spread_a = strew(item - 4, minus_a_ref[0:3])
        spread_b = strew(item - 3, minus_b_ref[0:3])
        minus_a = settle(item - 2, back_a_ref[...])
        minus_b = settle(item - 1, back_b_ref[...])
        pull_a = pull(item)
        pull_b = pull(item + 1)
        total_ref[...] = total_ref[...] + spread_a + spread_b
        minus_a_ref[0:3] = minus_a
        minus_b_ref[0:3] = minus_b
        back_a_ref[...] = pull_a
        back_b_ref[...] = pull_b
        return carry

    lax.fori_loop(0, rounds + 2, backward_round, 0)

    for tile in range(tiles):
        own_ref[:, tile * LANES : (tile + 1) * LANES] = own3_ref[tile]
    spread_ref[...] = jnp.zeros_like(spread_ref)
    for c in range(3):
        spread_ref[:, c, :] = total_ref[c * GROUP_ROWS : c * GROUP_ROWS + spread_ref.shape[0]]


def neighbours():
    found = []
    for axis in ("gx", "gy", "gz"):
        size = lax.axis_size(axis)
        place = lax.axis_index(axis)
        found.append({axis: lax.rem(place + 1, size)})
        found.append({axis: lax.rem(place + size - 1, size)})
    return found


def greet(found):
    barrier = pltpu.get_barrier_semaphore()
    for device in found:
        pl.semaphore_signal(
            barrier, inc=1, device_id=device, device_id_type=pl.DeviceIdType.MESH
        )
    pl.semaphore_wait(barrier, len(found))


FACES = ((0, 1, 1, 0), (0, 0, 0, 1), (1, 1, 3, 2), (1, 0, 2, 3), (2, 1, 5, 4), (2, 0, 4, 5))


def ready_weights(
    w1_ref,
    b1_ref,
    w2_ref,
    wo1_ref,
    wo2_ref,
    we1_ref,
    bf2_ref,
    bo1_ref,
    bo2_ref,
    be1_ref,
    w_e2_ref,
    square_ref,
    wide_ref,
    tall_ref,
    column_ref,
):
    radial, width = w1_ref.shape
    bias = b1_ref[...].reshape(1, width)
    bias_high = bias.astype(BF16).astype(F32)
    bias_middle = (bias - bias_high).astype(BF16).astype(F32)
    w1 = jnp.concatenate(
        [
            w1_ref[...].astype(F32),
            bias_high,
            bias_middle,
            bias - bias_high - bias_middle,
            jnp.zeros((RADIAL_ROWS - radial - 3, width), F32),
        ],
        axis=0,
    )
    radial_col = lax.broadcasted_iota(jnp.int32, (RADIAL_ROWS, 1), 0)
    tall_ref[0] = w1.T.astype(BF16)
    wide_ref[0] = jnp.where(radial_col < radial, w1, 0.0).astype(BF16)
    wide_ref[1] = we1_ref[...]
    tall_ref[1] = flip(we1_ref[...])
    for n, ref in enumerate((w2_ref, wo1_ref, wo2_ref)):
        square_ref[2 * n] = ref[...]
        square_ref[2 * n + 1] = flip(ref[...])
    ids = lax.broadcasted_iota(jnp.int32, (1, width), 1)
    rows = [
        bf2_ref[...].reshape(1, width) * LOG2E,
        bo1_ref[...].reshape(1, width),
        bo2_ref[...].reshape(1, width),
        ids.astype(F32) * (CUTOFF / (radial - 1)),
        jnp.where(ids < radial, -GAMMA * LOG2E, 0.0),
    ]
    for ref in (be1_ref, w_e2_ref):
        size = ref.shape[0]
        rows.append(
            jnp.concatenate(
                [ref[...].reshape(1, size), jnp.zeros((1, width - size), F32)], axis=1
            )
        )
    rows.append(jnp.zeros((width - len(rows), width), F32))
    column_ref[...] = jnp.concatenate(rows, axis=0).T


def prepare(
    lengths,
    held,
    feat_ref,
    disp_ref,
    index_ref,
    count_ref,
    species_ref,
    scale_ref,
    shift_ref,
    rows_ref,
    order_ref,
    counts_ref,
    vals_ref,
    sorted_ref,
    raw_ref,
    rank_ref,
):
    atoms = feat_ref.shape[0]
    slots = disp_ref.shape[1] // atoms
    tiles = atoms // LANES
    steps = slots // UNROLL
    idle = tiles * steps
    block = math.lcm(slots, LANES)
    lines = block // LANES
    each = block // slots
    groups = atoms // each

    raw_ref[...] = jnp.zeros_like(raw_ref)

    def lay(g, carry):
        for m in range(lines):
            at = pl.multiple_of((g * lines + m) * LANES, LANES)
            three = disp_ref[:, pl.ds(at, LANES)]
            for c in range(3):
                raw_ref[c, m, pl.ds(g, 1), :] = three[c : c + 1]
            line = index_ref[pl.ds(g * lines + m, 1), :]
            raw_ref[3, m, pl.ds(g, 1), :] = line.astype(F32)
        return carry

    lax.fori_loop(0, groups, lay, 0)

    atom_row = lax.broadcasted_iota(jnp.int32, (1, atoms), 1)
    atom_col = lax.broadcasted_iota(jnp.int32, (atoms, 1), 0)
    count_row = count_ref[...].reshape(1, atoms)
    key_row = (count_row * atoms - atom_row).astype(F32)
    count_col = jnp.broadcast_to(count_row.astype(F32), (128, atoms)).T[:, 0:1]
    key_col = count_col * float(atoms) - atom_col.astype(F32)
    rank_col = jnp.sum(jnp.where(key_row > key_col, 1.0, 0.0), axis=1, keepdims=True)
    perm = jnp.where(rank_col == atom_row.astype(F32), 1.0, 0.0).astype(BF16)

    rank_ref[...] = jnp.broadcast_to(rank_col, (atoms, LANES))
    order_ref[...] = rank_ref[...].T[0:8]
    lane_ids = lax.broadcasted_iota(jnp.int32, (groups, LANES), 1).astype(F32)
    blocks = []
    for a in range(each):
        rank = rank_ref[pl.ds(a, groups, stride=each), :]
        blocks.append(
            jnp.concatenate(
                [
                    jnp.where(rank - float(t * LANES) == lane_ids, 1.0, 0.0).astype(BF16)
                    for t in range(tiles)
                ],
                axis=1,
            )
        )
        if groups < LANES:
            blocks.append(jnp.zeros((LANES - groups, atoms), BF16))
    spots = jnp.concatenate(blocks, axis=0)

    def columns(c):
        turned = jnp.concatenate([raw_ref[c, m].T for m in range(lines)], axis=0)
        return jnp.concatenate(
            [turned[a * slots : (a + 1) * slots] for a in range(each)], axis=1
        )

    def put(ref, value):
        for tile in range(tiles):
            for s in range(steps):
                ref[tile * steps + s] = value[
                    s * UNROLL : (s + 1) * UNROLL, tile * LANES : (tile + 1) * LANES
                ]
        ref[idle] = jnp.zeros((UNROLL, LANES), F32)

    raw = jnp.concatenate([columns(c) for c in range(3)], axis=0)
    index = columns(3)
    index_high = jnp.floor(index * (1.0 / 128))
    index_low = index - index_high * 128.0
    stack = jnp.concatenate(
        list(split3(raw)) + [index_high.astype(BF16), index_low.astype(BF16)], axis=0
    )
    found = dot(stack, spots)
    size = 3 * slots
    disp = found[0:size] + found[size : 2 * size] + found[2 * size : 3 * size]
    row = found[3 * size : 3 * size + slots] * 128.0 + found[3 * size + slots : 3 * size + 2 * slots]
    put(rows_ref.at[0], row)
    packed = row
    edge = atoms
    for length, used in zip(lengths[:-1], held):
        edge += length
        packed = packed - jnp.where(row >= float(edge), float(length) - used.astype(F32), 0.0)
    put(rows_ref.at[8], packed)
    counts8 = dot(jnp.broadcast_to(count_row, (8, atoms)).astype(F32).astype(BF16), perm)
    counts = counts8[0:1]
    counts_ref[...] = counts8
    kinds = scale_ref.shape[0]
    kind_ids = lax.broadcasted_iota(jnp.int32, (kinds, 1), 0)
    kind_pick = jnp.where(kind_ids == species_ref[...].reshape(1, atoms), 1.0, 0.0).astype(BF16)
    pair_of = jnp.concatenate(
        [
            jnp.broadcast_to(scale_ref[...].reshape(1, kinds), (8, kinds)),
            jnp.broadcast_to(shift_ref[...].reshape(1, kinds), (8, kinds)),
        ],
        axis=0,
    )
    atom_vals = sum(dot(part, kind_pick) for part in split3(pair_of))
    vals_ref[...] = sum(dot(part, perm) for part in split3(atom_vals))
    sorted_ref[...] = dot(feat_ref[...].astype(F32).T.astype(BF16), perm).astype(BF16)

    dx = disp[0:slots]
    dy = disp[slots : 2 * slots]
    dz = disp[2 * slots : 3 * slots]
    squared = dx * dx + dy * dy + dz * dz
    distance = jnp.sqrt(squared)
    put(rows_ref.at[1], distance)
    slot_ids = lax.broadcasted_iota(jnp.int32, (slots, 1), 0).astype(F32)
    live = jnp.where(slot_ids < counts, 1.0, 0.0)
    y = (math.pi / CUTOFF) * distance - 0.5 * math.pi
    y2 = y * y
    sin_y = y * (
        1.0
        + y2
        * (
            -1.0 / 6
            + y2 * (1.0 / 120 + y2 * (-1.0 / 5040 + y2 * (1.0 / 362880 - y2 * (1.0 / 39916800))))
        )
    )
    envelope = (0.5 - 0.5 * sin_y) * live
    put(rows_ref.at[2], envelope)
    cos_y = 1.0 + y2 * (
        -0.5
        + y2
        * (
            1.0 / 24
            + y2
            * (
                -1.0 / 720
                + y2 * (1.0 / 40320 + y2 * (-1.0 / 3628800 + y2 * (1.0 / 479001600)))
            )
        )
    )
    inverse = live / distance
    put(rows_ref.at[3], envelope * (-2.0 * GAMMA) * inverse)
    put(rows_ref.at[4], (-0.5 * math.pi / CUTOFF * LOG_TWO) * cos_y * inverse)
    put(rows_ref.at[5], dx)
    put(rows_ref.at[6], dy)
    put(rows_ref.at[7], dz)


INPUTS = 23
OUTPUTS = 10


def named_faces(lists, used_ref):
    found = []
    used = used_ref[...]
    for dim, side, column, _ in FACES:
        names = lists[dim][side : side + 1, :]
        lanes = lax.broadcasted_iota(jnp.int32, names.shape, 1)
        found.append(jnp.where(lanes < used[:, column : column + 1], names, -1).astype(F32))
    return found


def send_kernel(*refs):
    far, refs = refs[:INPUTS], refs[INPUTS:]
    table_ref, results, refs = refs[0], refs[1 : OUTPUTS + 1], refs[OUTPUTS + 1 :]
    near, made, refs = refs[:INPUTS], refs[INPUTS : INPUTS + OUTPUTS], refs[INPUTS + OUTPUTS :]
    mine_ref, stage_ref, raw_ref, rank_ref, tag_ref, tags_ref, *sems = refs
    load_sem, save_sem, send_sem, recv_sem, tag_send_sem, tag_recv_sem = sems
    loads = [
        pltpu.make_async_copy(one, two, load_sem.at[n])
        for n, (one, two) in enumerate(zip(far, near))
    ]
    for load in loads:
        load.start()
    found = neighbours()
    greet(found)
    feat_ref, w_ref = near[0:2]
    used_here = near[5]
    atoms = feat_ref.shape[0]
    for load in loads[0:6]:
        load.wait()
    used = used_here[...]
    faces = used.shape[1]
    tag = jnp.concatenate([used, jnp.zeros((1, LANES - faces), jnp.int32)], axis=1)
    tag_ref[...] = jnp.broadcast_to(tag, tag_ref.shape)
    tags = []
    for n in range(faces):
        tag = pltpu.make_async_remote_copy(
            src_ref=tag_ref,
            dst_ref=tags_ref.at[n],
            send_sem=tag_send_sem.at[n],
            recv_sem=tag_recv_sem.at[n],
            device_id=found[n],
            device_id_type=pl.DeviceIdType.MESH,
        )
        tag.start()
        tags.append(tag)
    x_t = dot(feat_ref[...], w_ref[...]).T.astype(BF16)
    copies = []
    start = 0
    for n, names in enumerate(named_faces(near[2:5], near[5])):
        length = names.shape[1]
        stage_ref[:, start : start + length] = dot(x_t, one_hot(names, atoms)).astype(BF16)
        copy = pltpu.make_async_remote_copy(
            src_ref=stage_ref.at[:, pl.ds(start, length)],
            dst_ref=table_ref.at[:, pl.ds(atoms + start, length)],
            send_sem=send_sem.at[n],
            recv_sem=recv_sem.at[n],
            device_id=found[n],
            device_id_type=pl.DeviceIdType.MESH,
        )
        copy.start()
        copies.append(copy)
        start += length
    mine_ref[...] = x_t
    saves = [pltpu.make_async_copy(mine_ref, table_ref.at[:, pl.ds(0, atoms)], save_sem.at[0])]
    saves[0].start()
    for load in loads[6:]:
        load.wait()
    rows_ref, order_ref, counts_ref, vals_ref, sorted_ref = made[0:5]
    for tag in tags:
        tag.wait()
    held = [tags_ref[n, 0:1, face[2] : face[2] + 1] for n, face in enumerate(FACES)]
    made[-1][...] = jnp.concatenate(
        [jnp.broadcast_to(one, (1, LANES)) for one in held]
        + [jnp.zeros((8 - faces, LANES), jnp.int32)],
        axis=0,
    )
    lengths = [near[2 + face[0]].shape[1] for face in FACES]
    prepare(
        lengths,
        held,
        feat_ref,
        *near[6:12],
        rows_ref,
        order_ref,
        counts_ref,
        vals_ref,
        sorted_ref,
        raw_ref,
        rank_ref,
    )
    ready_weights(*near[12:], *made[5:9])
    for n, (one, two) in enumerate(zip(made, results)):
        save = pltpu.make_async_copy(one, two, save_sem.at[n + 1])
        save.start()
        saves.append(save)
    for copy in saves + copies:
        copy.wait()


def return_kernel(
    own_ref,
    spread_ref,
    order_ref,
    ex_ref,
    ey_ref,
    ez_ref,
    used_ref,
    force_ref,
    own_here,
    order_here,
    ex_here,
    ey_here,
    ez_here,
    used_here,
    mine_ref,
    land_ref,
    load_sem,
    send_sem,
    recv_sem,
):
    atoms = force_ref.shape[1]
    group = atoms // 128
    pairs = (
        (spread_ref.at[pl.ds(0, group)], mine_ref),
        (own_ref, own_here),
        (order_ref, order_here),
        (ex_ref, ex_here),
        (ey_ref, ey_here),
        (ez_ref, ez_here),
        (used_ref, used_here),
    )
    loads = [
        pltpu.make_async_copy(one, two, load_sem.at[n]) for n, (one, two) in enumerate(pairs)
    ]
    for load in loads:
        load.start()
    lists = (ex_here, ey_here, ez_here)
    found = neighbours()
    greet(found)
    copies = []
    start = 0
    for n, (dim, _, _, to) in enumerate(FACES):
        length = lists[dim].shape[1] // 128
        copy = pltpu.make_async_remote_copy(
            src_ref=spread_ref.at[pl.ds(group + start, length)],
            dst_ref=land_ref.at[pl.ds(start, length)],
            send_sem=send_sem.at[n],
            recv_sem=recv_sem.at[n],
            device_id=found[to ^ 1],
            device_id_type=pl.DeviceIdType.MESH,
        )
        copy.start()
        copies.append(copy)
        start += length
    for load in loads:
        load.wait()
    picks = jnp.concatenate(
        [one_hot(names, atoms) for names in named_faces(lists, used_here)], axis=1
    )
    total = jnp.concatenate([mine_ref[h] for h in range(group)], axis=1)
    part = dot(split2(own_here[...]), one_hot(order_here[0:1], atoms))
    total = total + part[0:8] + part[8:16]
    for copy in copies:
        copy.wait()
    values = jnp.concatenate([land_ref[h] for h in range(start)], axis=1)
    part = dot_nt(split2(values), picks)
    total = total + part[0:8] + part[8:16]
    force_ref[...] = total[0:3]


def body(
    features,
    displacement,
    neighbour,
    neighbour_count,
    species,
    exports_x,
    exports_y,
    exports_z,
    face_counts,
    w_in,
    w_f1,
    b_f1,
    w_f2,
    b_f2,
    w_o1,
    b_o1,
    w_o2,
    b_o2,
    w_e1,
    b_e1,
    w_e2,
    species_scale,
    species_shift,
):
    atom_rows, width = features.shape
    slot_count = neighbour.shape[0] // atom_rows
    vmem = pl.BlockSpec(memory_space=pltpu.VMEM)
    lists = (exports_x[0], exports_y[0], exports_z[0])
    ghost_rows = sum(2 * one.shape[1] for one in lists)
    table_rows = atom_rows + ghost_rows
    tiles = atom_rows // LANES
    steps = slot_count // UNROLL * tiles
    groups = table_rows // 128
    lines = math.lcm(slot_count, LANES) // LANES
    inputs = (
        features,
        w_in,
        *lists,
        face_counts,
        displacement,
        neighbour.reshape(-1, LANES),
        neighbour_count,
        species,
        species_scale,
        species_shift,
        w_f1,
        b_f1,
        w_f2,
        w_o1,
        w_o2,
        w_e1.T,
        b_f2,
        b_o1,
        b_o2,
        b_e1,
        w_e2,
    )
    hidden = w_e1.shape[1]
    anywhere = pl.BlockSpec(memory_space=pl.ANY)
    results = (
        jax.ShapeDtypeStruct((9, steps + 1, UNROLL, LANES), F32),
        jax.ShapeDtypeStruct((8, atom_rows), F32),
        jax.ShapeDtypeStruct((8, atom_rows), F32),
        jax.ShapeDtypeStruct((16, atom_rows), F32),
        jax.ShapeDtypeStruct((width, atom_rows), BF16),
        jax.ShapeDtypeStruct((6, width, width), BF16),
        jax.ShapeDtypeStruct((2, hidden, width), BF16),
        jax.ShapeDtypeStruct((2, width, hidden), BF16),
        jax.ShapeDtypeStruct((width, width), F32),
        jax.ShapeDtypeStruct((8, LANES), jnp.int32),
    )
    table_t, rows, order, counts, vals, sorted_t, *weights = pl.pallas_call(
        send_kernel,
        out_shape=(jax.ShapeDtypeStruct((width, table_rows), BF16),) + results,
        in_specs=[anywhere] * len(inputs),
        out_specs=(anywhere,) * (1 + len(results)),
        scratch_shapes=[pltpu.VMEM(one.shape, one.dtype) for one in inputs + results]
        + [
            pltpu.VMEM((width, atom_rows), BF16),
            pltpu.VMEM((width, ghost_rows), BF16),
            pltpu.VMEM((4, lines, LANES, LANES), F32),
            pltpu.VMEM((atom_rows, LANES), F32),
            pltpu.VMEM((8, LANES), jnp.int32),
            pltpu.VMEM((6, 8, LANES), jnp.int32),
            pltpu.SemaphoreType.DMA((len(inputs),)),
            pltpu.SemaphoreType.DMA((1 + len(results),)),
            pltpu.SemaphoreType.DMA((6,)),
            pltpu.SemaphoreType.DMA((6,)),
            pltpu.SemaphoreType.DMA((6,)),
            pltpu.SemaphoreType.DMA((6,)),
        ],
        compiler_params=pltpu.CompilerParams(
            collective_id=0, has_side_effects=True, vmem_limit_bytes=58 * 1024 * 1024
        ),
    )(*inputs)
    span = UNROLL * LANES
    energy, own_force, spread = pl.pallas_call(
        functools.partial(pair_kernel, [one.shape[1] for one in lists for _ in range(2)]),
        out_shape=(
            jax.ShapeDtypeStruct((atom_rows,), F32),
            jax.ShapeDtypeStruct((8, atom_rows), F32),
            jax.ShapeDtypeStruct((groups, 8, 128), F32),
        ),
        in_specs=[vmem] * 10 + [pl.BlockSpec(memory_space=pltpu.SMEM)],
        out_specs=(vmem, vmem, vmem),
        scratch_shapes=[
            pltpu.VMEM((tiles, width, LANES), F32),
            pltpu.VMEM((tiles, width, LANES), F32),
            pltpu.VMEM((tiles, 8, LANES), F32),
            pltpu.VMEM((steps + 10, width, span), BF16),
            pltpu.VMEM((steps + 10, width, span), BF16),
            pltpu.VMEM((steps + 10, width, span), BF16),
            pltpu.VMEM((steps + 10, RADIAL_ROWS, span), BF16),
            pltpu.VMEM((width, span), BF16),
            pltpu.VMEM((width, span), BF16),
            pltpu.VMEM((width, span), F32),
            pltpu.VMEM((width, span), F32),
            pltpu.VMEM((width, span), F32),
            pltpu.VMEM((width, span), F32),
            pltpu.VMEM((width, span), BF16),
            pltpu.VMEM((width, span), BF16),
            pltpu.VMEM((8, span), F32),
            pltpu.VMEM((8, span), F32),
            pltpu.VMEM((3 * GROUP_ROWS, 128), F32),
            pltpu.VMEM((width, -(-table_rows // CHUNK) * CHUNK + LANES), BF16),
        ],
        compiler_params=pltpu.CompilerParams(vmem_limit_bytes=58 * 1024 * 1024),
        cost_estimate=pl.CostEstimate(
            flops=30_000_000_000, bytes_accessed=4_000_000, transcendentals=16_000_000
        ),
    )(
        rows,
        order,
        counts,
        vals,
        sorted_t,
        table_t,
        *weights,
    )
    last = (own_force, spread, order, *lists, face_counts)
    copied = (own_force, order, *lists, face_counts)
    forces = pl.pallas_call(
        return_kernel,
        out_shape=jax.ShapeDtypeStruct((3, atom_rows), F32),
        in_specs=[anywhere] * len(last),
        out_specs=vmem,
        scratch_shapes=[pltpu.VMEM(one.shape, one.dtype) for one in copied]
        + [
            pltpu.VMEM((tiles, 8, LANES), F32),
            pltpu.VMEM((ghost_rows // 128, 8, 128), F32),
            pltpu.SemaphoreType.DMA((len(last),)),
            pltpu.SemaphoreType.DMA((6,)),
            pltpu.SemaphoreType.DMA((6,)),
        ],
        compiler_params=pltpu.CompilerParams(
            collective_id=1, has_side_effects=True, vmem_limit_bytes=58 * 1024 * 1024
        ),
    )(*last)
    return (energy, forces)


def solution(mesh):
    both = ("geom", "gx", "gy", "gz")
    return jax.shard_map(
        body,
        mesh=mesh,
        in_specs=(
            P(both, None),
            P(None, both),
            P(both),
            P(both),
            P(both),
            P(both, None, None),
            P(both, None, None),
            P(both, None, None),
            P(both, None),
        )
        + (P(),) * 14,
        out_specs=(P(both), P(None, both)),
        check_vma=False,
    )
```

```python
import functools
import math

import jax
import jax.numpy as jnp
from jax import lax
from jax.experimental import pallas as pl
from jax.experimental.pallas import tpu as pltpu
from jax.sharding import PartitionSpec as P

GAMMA = 10.0
CUTOFF = 5.0
LOG_TWO = math.log(2.0)
LOG2E = 1.0 / LOG_TWO
LANES = 128
UNROLL = 4
CHUNK = 256
RADIAL_ROWS = 64
GROUP_ROWS = 32
BEHIND = 2

BF16 = jnp.bfloat16
F32 = jnp.float32


def dot(a, b):
    return jnp.dot(a, b, preferred_element_type=F32)


def dot_nt(a, b):
    return lax.dot_general(a, b, (((1,), (1,)), ((), ())), preferred_element_type=F32)


def split3(value):
    high = value.astype(BF16)
    rest = value - high.astype(F32)
    middle = rest.astype(BF16)
    low = (rest - middle.astype(F32)).astype(BF16)
    return high, middle, low


def split2(value):
    high = value.astype(BF16)
    low = (value - high.astype(F32)).astype(BF16)
    return jnp.concatenate([high, low], axis=0)


def softplus_of(value):
    return jnp.maximum(value, 0.0) + jnp.log(1.0 + jnp.exp(-jnp.abs(value)))


def sigmoid_of(value):
    return 1.0 / (1.0 + jnp.exp(-value))


def one_hot(row, size):
    span = row.shape[1]
    parts = []
    for start in range(0, size, CHUNK):
        spot = jnp.broadcast_to(row - float(start), (16, span)).astype(BF16)
        lanes = lax.broadcasted_iota(jnp.int32, (16, span), 0).astype(F32)
        for b in range(min(CHUNK, size - start) // 16):
            ids = (lanes + float(16 * b)).astype(BF16)
            parts.append(jnp.where(ids == spot, jnp.ones((), BF16), jnp.zeros((), BF16)))
    return jnp.concatenate(parts, axis=0)


def flip(weight):
    return weight.astype(F32).T.astype(BF16)


def packed_height(length):
    return -(-3 * (length // LANES) // 8) * 8


def unpacked(ref, at, length):
    count = length // LANES
    return jnp.concatenate(
        [
            jnp.concatenate(
                [ref[at + c * count + h : at + c * count + h + 1] for h in range(count)], axis=1
            )
            for c in range(3)
        ]
        + [jnp.zeros((5, length), F32)],
        axis=0,
    )


def pair_kernel(
    lengths,
    rows_ref,
    order_ref,
    counts_ref,
    vals_ref,
    feat_ref,
    table_ref,
    square_ref,
    wide_ref,
    tall_ref,
    column_ref,
    held_ref,
    energy_ref,
    spread_ref,
    msg_ref,
    gm_ref,
    own3_ref,
    xj_ref,
    prod_ref,
    sig_ref,
    slope_ref,
    hid_a_ref,
    hid_b_ref,
    filt_a_ref,
    filt_b_ref,
    found_a_ref,
    found_b_ref,
    back_a_ref,
    back_b_ref,
    minus_a_ref,
    minus_b_ref,
    total_ref,
    packed_ref,
):
    width, atoms = feat_ref.shape
    tiles = atoms // LANES
    steps = (rows_ref.shape[1] - 1) // tiles
    span = UNROLL * LANES
    table_rows = table_ref.shape[1]
    idle = tiles * steps

    counts = counts_ref[0:1]
    scale = vals_ref[0:1]
    shift = vals_ref[8:9]
    feat = feat_ref[...].astype(F32)
    row_ref, dist_ref, env_ref, near_ref, far_ref = [rows_ref.at[n] for n in range(5)]

    w2, w2t, wo1, wo1t, wo2, wo2t = [square_ref[n] for n in range(6)]
    w1_back, we1 = wide_ref[0], wide_ref[1]
    w1t, we1t = tall_ref[0], tall_ref[1]
    b_f2, b_o1, b_o2, mu, sharp = [column_ref[:, n : n + 1] for n in range(5)]
    mu, sharp = mu[0:RADIAL_ROWS], sharp[0:RADIAL_ROWS]
    b_e1, w_e2 = [column_ref[0 : we1.shape[0], n : n + 1] for n in (5, 6)]

    def lane_row(ref, at):
        return jnp.concatenate([ref[at, u : u + 1, :] for u in range(UNROLL)], axis=1)

    ends = []
    items = jnp.zeros((), jnp.int32)
    for tile in range(tiles):
        most = jnp.max(counts[:, tile * LANES : (tile + 1) * LANES]).astype(jnp.int32)
        items = items + (most + (UNROLL - 1)) // UNROLL
        ends.append(items)
    rounds = (items + 1) // 2
    turns = (items + 3) // 4

    def place(item):
        tile = jnp.zeros((), jnp.int32)
        first = jnp.zeros((), jnp.int32)
        for end in ends[:-1]:
            past = item >= end
            tile = tile + past.astype(jnp.int32)
            first = jnp.where(past, end, first)
        at = jnp.where((item >= 0) & (item < items), tile * steps + item - first, idle)
        return tile, at

    packed_ref[...] = jnp.zeros_like(packed_ref)
    packed_ref[:, 0:atoms] = table_ref[:, 0:atoms]
    lane_ids = lax.broadcasted_iota(jnp.int32, (width, LANES), 1)
    packed_rows = jnp.full((), atoms, jnp.int32)
    edge = atoms
    for n, length in enumerate(lengths):
        turn = packed_rows & (LANES - 1)
        base = packed_rows - turn
        below = lane_ids < turn
        first = pl.multiple_of(base, LANES)
        last = packed_ref[:, pl.ds(first, LANES)].astype(F32)
        for t in range(length // LANES):
            slab = table_ref[:, edge + t * LANES : edge + (t + 1) * LANES].astype(F32)
            slab = pltpu.roll(slab, turn, 1)
            at = pl.multiple_of(base + t * LANES, LANES)
            packed_ref[:, pl.ds(at, LANES)] = jnp.where(below, last, slab).astype(BF16)
            last = slab
        at = pl.multiple_of(base + length, LANES)
        packed_ref[:, pl.ds(at, LANES)] = jnp.where(below, last, 0.0).astype(BF16)
        packed_rows = packed_rows + held_ref[n, 0]
        edge += length

    def radial_dot(at):
        offset = lane_row(dist_ref, at) - mu
        basis = jnp.exp2(sharp * (offset * offset))
        return (offset * basis).astype(BF16), dot(w1t, basis.astype(BF16))

    def activate(pre):
        grown = jnp.exp2(pre * LOG2E)
        total = 1.0 + grown
        sig = (grown * pl.reciprocal(total, approx=True)).astype(BF16)
        return sig, (jnp.log2(total) - 1.0).astype(BF16)

    def begin(item, hid_ref):
        slope, pre = radial_dot(place(item)[1])
        slope_ref[item + BEHIND] = slope
        sig, hidden = activate(pre)
        sig_ref[item + BEHIND] = sig
        hid_ref[...] = hidden

    def finish(item, filt_ref, found_ref):
        tile, at = place(item)
        prod = found_ref[...] * filt_ref[...]
        prod_ref[item + BEHIND] = prod.astype(BF16)
        weighted = prod * lane_row(env_ref, at)
        part = msg_ref[tile]
        for u in range(UNROLL):
            part = part + weighted[:, u * LANES : (u + 1) * LANES]
        msg_ref[tile] = part

    def forward(size, item, hid_ref, next_ref, filt_ref, found_ref, last_filt_ref, last_found_ref):
        filt = dot(w2t, hid_ref[...]) + b_f2
        slope, pre = radial_dot(place(item + 1)[1])
        slope_ref[item + BEHIND + 1] = slope
        picked = one_hot(lane_row(rows_ref.at[8], place(item)[1]), size)
        found = dot(packed_ref[:, 0:size], picked)
        sig, hidden = activate(pre)
        sig_ref[item + BEHIND + 1] = sig
        next_ref[...] = hidden
        finish(item - 1, last_filt_ref, last_found_ref)
        filt_ref[...] = filt
        found_ref[...] = found
        xj_ref[item + BEHIND] = found.astype(BF16)

    msg_ref[...] = jnp.zeros_like(msg_ref)
    filt_b_ref[...] = jnp.zeros_like(filt_b_ref)
    found_b_ref[...] = jnp.zeros_like(found_b_ref)
    begin(jnp.zeros((), jnp.int32), hid_a_ref)

    def forward_all(size):
        def forward_round(turn, carry):
            a = (filt_a_ref, found_a_ref)
            b = (filt_b_ref, found_b_ref)
            for n in range(0, 4, 2):
                item = 4 * turn + n
                forward(size, item, hid_a_ref, hid_b_ref, *a, *b)
                forward(size, item + 1, hid_b_ref, hid_a_ref, *b, *a)
            return carry

        lax.fori_loop(0, turns, forward_round, 0)

    most = -(-table_rows // CHUNK) * CHUNK
    sizes = [size for size in range(most - 3 * CHUNK, most + 1, CHUNK) if size > 0]
    for n, size in enumerate(sizes):
        fits = packed_rows <= size
        if n:
            fits = fits & (packed_rows > sizes[n - 1])

        @pl.when(fits)
        def _(size=size):
            forward_all(size)

    finish(4 * turns - 1, filt_b_ref, found_b_ref)

    message = jnp.concatenate([msg_ref[t] for t in range(tiles)], axis=1)
    message = (message * LOG_TWO).astype(BF16)
    out_pre = dot(wo1t, message) + b_o1
    out_mid = (softplus_of(out_pre) - LOG_TWO).astype(BF16)
    updated = (feat + dot(wo2t, out_mid) + b_o2).astype(BF16)
    energy_pre = dot(we1, updated) + b_e1
    soft = softplus_of(energy_pre) - LOG_TWO
    energy = scale * jnp.sum(soft * w_e2, axis=0, keepdims=True) + shift
    home = one_hot(order_ref[0:1], atoms)
    plain = dot(split2(jnp.broadcast_to(energy, (8, atoms))), home)
    energy_ref[...] = (plain[0:1] + plain[8:9]).reshape(atoms)
    grad_head = (scale * w_e2 * sigmoid_of(energy_pre)).astype(BF16)
    grad_update = dot(we1t, grad_head).astype(BF16)
    grad_mid = (dot(wo2, grad_update) * sigmoid_of(out_pre)).astype(BF16)
    grad_message = dot(wo1, grad_mid)
    for tile in range(tiles):
        gm_ref[tile] = grad_message[:, tile * LANES : (tile + 1) * LANES]

    total_ref[...] = jnp.zeros_like(total_ref)
    own3_ref[...] = jnp.zeros_like(own3_ref)
    for ref in (back_a_ref, back_b_ref, minus_a_ref, minus_b_ref):
        ref[...] = jnp.zeros_like(ref)
    for early in range(BEHIND):
        prod_ref[early] = jnp.zeros((width, span), BF16)
        slope_ref[early] = jnp.zeros((RADIAL_ROWS, span), BF16)
    for late in range(4):
        ahead = 2 * rounds + BEHIND + late
        xj_ref[ahead] = jnp.zeros((width, span), BF16)
        prod_ref[ahead] = jnp.zeros((width, span), BF16)
        slope_ref[ahead] = jnp.zeros((RADIAL_ROWS, span), BF16)
        sig_ref[ahead] = jnp.zeros((width, span), BF16)

    def pull(item):
        tile, at = place(item)
        grad_b = gm_ref[tile].astype(BF16)
        grad_b_wide = jnp.concatenate([grad_b] * UNROLL, axis=1)
        mixed = dot(w2, grad_b_wide * xj_ref[item + BEHIND])
        return (mixed * sig_ref[item + BEHIND].astype(F32)).astype(BF16)

    def settle(item, grad_pre):
        tile, at = place(item)
        grad_basis = dot(w1_back, grad_pre)
        grad_wide = jnp.concatenate([gm_ref[tile]] * UNROLL, axis=1)
        s1 = jnp.sum(grad_basis * slope_ref[item + BEHIND].astype(F32), axis=0, keepdims=True)
        s2 = jnp.sum(grad_wide * prod_ref[item + BEHIND].astype(F32), axis=0, keepdims=True)
        ratio = s1 * lane_row(near_ref, at) + s2 * lane_row(far_ref, at)
        forces = []
        for c in range(3):
            force = ratio * lane_row(rows_ref.at[5 + c], at)
            part = own3_ref[tile, c : c + 1, :]
            for u in range(UNROLL):
                part = part + force[:, u * LANES : (u + 1) * LANES]
            own3_ref[tile, c : c + 1, :] = part
            forces.append(-force)
        return jnp.concatenate(forces, axis=0)

    def strew(item, minus):
        row = lane_row(row_ref, place(item)[1])
        high = jnp.floor(row * (1.0 / 128))
        low = row - high * 128.0
        wide = (16, span)
        high_b = jnp.broadcast_to(high, wide).astype(BF16)
        low_b = jnp.broadcast_to(low, wide).astype(BF16)
        lanes = lax.broadcasted_iota(jnp.int32, wide, 0).astype(F32)
        ids = [(lanes + float(16 * b)).astype(BF16) for b in range(8)]
        lower = jnp.concatenate(
            [jnp.where(one == low_b, jnp.ones((), BF16), jnp.zeros((), BF16)) for one in ids],
            axis=0,
        )
        here = [ids[b] == high_b for b in range(GROUP_ROWS // 16)]
        placed = []
        for c in range(3):
            part = jnp.broadcast_to(minus[c : c + 1], wide).astype(BF16)
            placed += [jnp.where(mask, part, jnp.zeros((), BF16)) for mask in here]
        return dot_nt(jnp.concatenate(placed, axis=0), lower)

    def backward_round(turn, carry):
        item = 2 * turn
        spread_a = strew(item - 4, minus_a_ref[0:3])
        spread_b = strew(item - 3, minus_b_ref[0:3])
        minus_a = settle(item - 2, back_a_ref[...])
        minus_b = settle(item - 1, back_b_ref[...])
        pull_a = pull(item)
        pull_b = pull(item + 1)
        total_ref[...] = total_ref[...] + spread_a + spread_b
        minus_a_ref[0:3] = minus_a
        minus_b_ref[0:3] = minus_b
        back_a_ref[...] = pull_a
        back_b_ref[...] = pull_b
        return carry

    lax.fori_loop(0, rounds + 2, backward_round, 0)

    spread_ref[...] = jnp.zeros_like(spread_ref)
    group = tiles
    at = 0
    for length in [atoms] + list(lengths):
        count = length // LANES
        first = 0 if at == 0 else group
        for c in range(3):
            rows = total_ref[c * GROUP_ROWS + first : c * GROUP_ROWS + first + count]
            spread_ref[at + c * count : at + (c + 1) * count] = rows
        group = group + count if at else group
        at += packed_height(length)
    for tile in range(tiles):
        spread_ref[at + 8 * tile : at + 8 * tile + 8] = own3_ref[tile]


def neighbours():
    found = []
    for axis in ("gx", "gy", "gz"):
        size = lax.axis_size(axis)
        place = lax.axis_index(axis)
        found.append({axis: lax.rem(place + 1, size)})
        found.append({axis: lax.rem(place + size - 1, size)})
    return found


def greet(found):
    barrier = pltpu.get_barrier_semaphore()
    for device in found:
        pl.semaphore_signal(
            barrier, inc=1, device_id=device, device_id_type=pl.DeviceIdType.MESH
        )
    pl.semaphore_wait(barrier, len(found))


FACES = ((0, 1, 1, 0), (0, 0, 0, 1), (1, 1, 3, 2), (1, 0, 2, 3), (2, 1, 5, 4), (2, 0, 4, 5))


def ready_weights(
    w1_ref,
    b1_ref,
    w2_ref,
    wo1_ref,
    wo2_ref,
    we1_ref,
    bf2_ref,
    bo1_ref,
    bo2_ref,
    be1_ref,
    w_e2_ref,
    square_ref,
    wide_ref,
    tall_ref,
    column_ref,
):
    radial, width = w1_ref.shape
    bias = b1_ref[...].reshape(1, width)
    bias_high = bias.astype(BF16).astype(F32)
    bias_middle = (bias - bias_high).astype(BF16).astype(F32)
    w1 = jnp.concatenate(
        [
            w1_ref[...].astype(F32),
            bias_high,
            bias_middle,
            bias - bias_high - bias_middle,
            jnp.zeros((RADIAL_ROWS - radial - 3, width), F32),
        ],
        axis=0,
    )
    radial_col = lax.broadcasted_iota(jnp.int32, (RADIAL_ROWS, 1), 0)
    tall_ref[0] = w1.T.astype(BF16)
    wide_ref[0] = jnp.where(radial_col < radial, w1, 0.0).astype(BF16)
    wide_ref[1] = we1_ref[...]
    tall_ref[1] = flip(we1_ref[...])
    for n, ref in enumerate((w2_ref, wo1_ref, wo2_ref)):
        square_ref[2 * n] = ref[...]
        square_ref[2 * n + 1] = flip(ref[...])
    ids = lax.broadcasted_iota(jnp.int32, (1, width), 1)
    rows = [
        bf2_ref[...].reshape(1, width) * LOG2E,
        bo1_ref[...].reshape(1, width),
        bo2_ref[...].reshape(1, width),
        ids.astype(F32) * (CUTOFF / (radial - 1)),
        jnp.where(ids < radial, -GAMMA * LOG2E, 0.0),
    ]
    for ref in (be1_ref, w_e2_ref):
        size = ref.shape[0]
        rows.append(
            jnp.concatenate(
                [ref[...].reshape(1, size), jnp.zeros((1, width - size), F32)], axis=1
            )
        )
    rows.append(jnp.zeros((width - len(rows), width), F32))
    column_ref[...] = jnp.concatenate(rows, axis=0).T


def prepare(
    lengths,
    held,
    feat_ref,
    disp_ref,
    index_ref,
    count_ref,
    species_ref,
    scale_ref,
    shift_ref,
    rows_ref,
    order_ref,
    counts_ref,
    vals_ref,
    sorted_ref,
    raw_ref,
    rank_ref,
):
    atoms = feat_ref.shape[0]
    slots = disp_ref.shape[1] // atoms
    tiles = atoms // LANES
    steps = slots // UNROLL
    idle = tiles * steps
    block = math.lcm(slots, LANES)
    lines = block // LANES
    each = block // slots
    groups = atoms // each

    raw_ref[...] = jnp.zeros_like(raw_ref)

    def lay(g, carry):
        for m in range(lines):
            at = pl.multiple_of((g * lines + m) * LANES, LANES)
            three = disp_ref[:, pl.ds(at, LANES)]
            for c in range(3):
                raw_ref[c, m, pl.ds(g, 1), :] = three[c : c + 1]
            line = index_ref[pl.ds(g * lines + m, 1), :]
            raw_ref[3, m, pl.ds(g, 1), :] = line.astype(F32)
        return carry

    lax.fori_loop(0, groups, lay, 0)

    atom_row = lax.broadcasted_iota(jnp.int32, (1, atoms), 1)
    atom_col = lax.broadcasted_iota(jnp.int32, (atoms, 1), 0)
    count_row = count_ref[...].reshape(1, atoms)
    key_row = (count_row * atoms - atom_row).astype(F32)
    count_col = jnp.broadcast_to(count_row.astype(F32), (128, atoms)).T[:, 0:1]
    key_col = count_col * float(atoms) - atom_col.astype(F32)
    rank_col = jnp.sum(jnp.where(key_row > key_col, 1.0, 0.0), axis=1, keepdims=True)
    perm = jnp.where(rank_col == atom_row.astype(F32), 1.0, 0.0).astype(BF16)

    rank_ref[...] = jnp.broadcast_to(rank_col, (atoms, LANES))
    order_ref[...] = rank_ref[...].T[0:8]
    lane_ids = lax.broadcasted_iota(jnp.int32, (groups, LANES), 1).astype(F32)
    blocks = []
    for a in range(each):
        rank = rank_ref[pl.ds(a, groups, stride=each), :]
        blocks.append(
            jnp.concatenate(
                [
                    jnp.where(rank - float(t * LANES) == lane_ids, 1.0, 0.0).astype(BF16)
                    for t in range(tiles)
                ],
                axis=1,
            )
        )
        if groups < LANES:
            blocks.append(jnp.zeros((LANES - groups, atoms), BF16))
    spots = jnp.concatenate(blocks, axis=0)

    def columns(c):
        turned = jnp.concatenate([raw_ref[c, m].T for m in range(lines)], axis=0)
        return jnp.concatenate(
            [turned[a * slots : (a + 1) * slots] for a in range(each)], axis=1
        )

    def put(ref, value):
        for tile in range(tiles):
            for s in range(steps):
                ref[tile * steps + s] = value[
                    s * UNROLL : (s + 1) * UNROLL, tile * LANES : (tile + 1) * LANES
                ]
        ref[idle] = jnp.zeros((UNROLL, LANES), F32)

    raw = jnp.concatenate([columns(c) for c in range(3)], axis=0)
    index = columns(3)
    index_high = jnp.floor(index * (1.0 / 128))
    index_low = index - index_high * 128.0
    stack = jnp.concatenate(
        list(split3(raw)) + [index_high.astype(BF16), index_low.astype(BF16)], axis=0
    )
    found = dot(stack, spots)
    size = 3 * slots
    disp = found[0:size] + found[size : 2 * size] + found[2 * size : 3 * size]
    row = found[3 * size : 3 * size + slots] * 128.0 + found[3 * size + slots : 3 * size + 2 * slots]
    put(rows_ref.at[0], row)
    packed = row
    edge = atoms
    for length, used in zip(lengths[:-1], held):
        edge += length
        packed = packed - jnp.where(row >= float(edge), float(length) - used.astype(F32), 0.0)
    put(rows_ref.at[8], packed)
    counts8 = dot(jnp.broadcast_to(count_row, (8, atoms)).astype(F32).astype(BF16), perm)
    counts = counts8[0:1]
    counts_ref[...] = counts8
    kinds = scale_ref.shape[0]
    kind_ids = lax.broadcasted_iota(jnp.int32, (kinds, 1), 0)
    kind_pick = jnp.where(kind_ids == species_ref[...].reshape(1, atoms), 1.0, 0.0).astype(BF16)
    pair_of = jnp.concatenate(
        [
            jnp.broadcast_to(scale_ref[...].reshape(1, kinds), (8, kinds)),
            jnp.broadcast_to(shift_ref[...].reshape(1, kinds), (8, kinds)),
        ],
        axis=0,
    )
    atom_vals = sum(dot(part, kind_pick) for part in split3(pair_of))
    vals_ref[...] = sum(dot(part, perm) for part in split3(atom_vals))
    sorted_ref[...] = dot(feat_ref[...].astype(F32).T.astype(BF16), perm).astype(BF16)

    dx = disp[0:slots]
    dy = disp[slots : 2 * slots]
    dz = disp[2 * slots : 3 * slots]
    squared = dx * dx + dy * dy + dz * dz
    distance = jnp.sqrt(squared)
    put(rows_ref.at[1], distance)
    slot_ids = lax.broadcasted_iota(jnp.int32, (slots, 1), 0).astype(F32)
    live = jnp.where(slot_ids < counts, 1.0, 0.0)
    y = (math.pi / CUTOFF) * distance - 0.5 * math.pi
    y2 = y * y
    sin_y = y * (
        1.0
        + y2
        * (
            -1.0 / 6
            + y2 * (1.0 / 120 + y2 * (-1.0 / 5040 + y2 * (1.0 / 362880 - y2 * (1.0 / 39916800))))
        )
    )
    envelope = (0.5 - 0.5 * sin_y) * live
    put(rows_ref.at[2], envelope)
    cos_y = 1.0 + y2 * (
        -0.5
        + y2
        * (
            1.0 / 24
            + y2
            * (
                -1.0 / 720
                + y2 * (1.0 / 40320 + y2 * (-1.0 / 3628800 + y2 * (1.0 / 479001600)))
            )
        )
    )
    inverse = live / distance
    put(rows_ref.at[3], envelope * (-2.0 * GAMMA) * inverse)
    put(rows_ref.at[4], (-0.5 * math.pi / CUTOFF * LOG_TWO) * cos_y * inverse)
    put(rows_ref.at[5], dx)
    put(rows_ref.at[6], dy)
    put(rows_ref.at[7], dz)


INPUTS = 23
OUTPUTS = 10


def named_faces(lists, used_ref):
    found = []
    used = used_ref[...]
    for dim, side, column, _ in FACES:
        names = lists[dim][side : side + 1, :]
        lanes = lax.broadcasted_iota(jnp.int32, names.shape, 1)
        found.append(jnp.where(lanes < used[:, column : column + 1], names, -1).astype(F32))
    return found


def send_kernel(*refs):
    far, refs = refs[:INPUTS], refs[INPUTS:]
    table_ref, results, refs = refs[0], refs[1 : OUTPUTS + 1], refs[OUTPUTS + 1 :]
    near, made, refs = refs[:INPUTS], refs[INPUTS : INPUTS + OUTPUTS], refs[INPUTS + OUTPUTS :]
    mine_ref, stage_ref, raw_ref, rank_ref, tag_ref, tags_ref, *sems = refs
    load_sem, save_sem, send_sem, recv_sem, tag_send_sem, tag_recv_sem = sems
    loads = [
        pltpu.make_async_copy(one, two, load_sem.at[n])
        for n, (one, two) in enumerate(zip(far, near))
    ]
    for load in loads:
        load.start()
    found = neighbours()
    greet(found)
    feat_ref, w_ref = near[0:2]
    used_here = near[5]
    atoms = feat_ref.shape[0]
    for load in loads[0:6]:
        load.wait()
    used = used_here[...]
    faces = used.shape[1]
    tag = jnp.concatenate([used, jnp.zeros((1, LANES - faces), jnp.int32)], axis=1)
    tag_ref[...] = jnp.broadcast_to(tag, tag_ref.shape)
    tags = []
    for n in range(faces):
        tag = pltpu.make_async_remote_copy(
            src_ref=tag_ref,
            dst_ref=tags_ref.at[n],
            send_sem=tag_send_sem.at[n],
            recv_sem=tag_recv_sem.at[n],
            device_id=found[n],
            device_id_type=pl.DeviceIdType.MESH,
        )
        tag.start()
        tags.append(tag)
    x_t = dot(feat_ref[...], w_ref[...]).T.astype(BF16)
    copies = []
    start = 0
    for n, names in enumerate(named_faces(near[2:5], near[5])):
        length = names.shape[1]
        stage_ref[:, start : start + length] = dot(x_t, one_hot(names, atoms)).astype(BF16)
        copy = pltpu.make_async_remote_copy(
            src_ref=stage_ref.at[:, pl.ds(start, length)],
            dst_ref=table_ref.at[:, pl.ds(atoms + start, length)],
            send_sem=send_sem.at[n],
            recv_sem=recv_sem.at[n],
            device_id=found[n],
            device_id_type=pl.DeviceIdType.MESH,
        )
        copy.start()
        copies.append(copy)
        start += length
    mine_ref[...] = x_t
    saves = [pltpu.make_async_copy(mine_ref, table_ref.at[:, pl.ds(0, atoms)], save_sem.at[0])]
    saves[0].start()
    for load in loads[6:]:
        load.wait()
    rows_ref, order_ref, counts_ref, vals_ref, sorted_ref = made[0:5]
    for tag in tags:
        tag.wait()
    held = [tags_ref[n, 0:1, face[2] : face[2] + 1] for n, face in enumerate(FACES)]
    made[-1][...] = jnp.concatenate(
        [jnp.broadcast_to(one, (1, LANES)) for one in held]
        + [jnp.zeros((8 - faces, LANES), jnp.int32)],
        axis=0,
    )
    lengths = [near[2 + face[0]].shape[1] for face in FACES]
    prepare(
        lengths,
        held,
        feat_ref,
        *near[6:12],
        rows_ref,
        order_ref,
        counts_ref,
        vals_ref,
        sorted_ref,
        raw_ref,
        rank_ref,
    )
    ready_weights(*near[12:], *made[5:9])
    for n, (one, two) in enumerate(zip(made, results)):
        save = pltpu.make_async_copy(one, two, save_sem.at[n + 1])
        save.start()
        saves.append(save)
    for copy in saves + copies:
        copy.wait()


def return_kernel(
    spread_ref,
    order_ref,
    ex_ref,
    ey_ref,
    ez_ref,
    used_ref,
    force_ref,
    order_here,
    ex_here,
    ey_here,
    ez_here,
    used_here,
    mine_ref,
    land_ref,
    load_sem,
    send_sem,
    recv_sem,
):
    atoms = force_ref.shape[1]
    pairs = (
        (spread_ref, mine_ref),
        (order_ref, order_here),
        (ex_ref, ex_here),
        (ey_ref, ey_here),
        (ez_ref, ez_here),
        (used_ref, used_here),
    )
    loads = [
        pltpu.make_async_copy(one, two, load_sem.at[n]) for n, (one, two) in enumerate(pairs)
    ]
    for load in loads:
        load.start()
    lists = (ex_here, ey_here, ez_here)
    found = neighbours()
    greet(found)
    base = packed_height(atoms)
    places = []
    copies = []
    start = 0
    for n, (dim, _, _, to) in enumerate(FACES):
        places.append((start, lists[dim].shape[1]))
        length = packed_height(lists[dim].shape[1])
        copy = pltpu.make_async_remote_copy(
            src_ref=spread_ref.at[pl.ds(base + start, length)],
            dst_ref=land_ref.at[pl.ds(start, length)],
            send_sem=send_sem.at[n],
            recv_sem=recv_sem.at[n],
            device_id=found[to ^ 1],
            device_id_type=pl.DeviceIdType.MESH,
        )
        copy.start()
        copies.append(copy)
        start += length
    for load in loads:
        load.wait()
    picks = jnp.concatenate(
        [one_hot(names, atoms) for names in named_faces(lists, used_here)], axis=1
    )
    total = unpacked(mine_ref, 0, atoms)
    own = base + start
    own = [mine_ref[own + 8 * t : own + 8 * t + 8] for t in range(atoms // LANES)]
    part = dot(split2(jnp.concatenate(own, axis=1)), one_hot(order_here[0:1], atoms))
    total = total + part[0:8] + part[8:16]
    for copy in copies:
        copy.wait()
    values = jnp.concatenate([unpacked(land_ref, *place) for place in places], axis=1)
    part = dot_nt(split2(values), picks)
    total = total + part[0:8] + part[8:16]
    force_ref[...] = total[0:3]


def body(
    features,
    displacement,
    neighbour,
    neighbour_count,
    species,
    exports_x,
    exports_y,
    exports_z,
    face_counts,
    w_in,
    w_f1,
    b_f1,
    w_f2,
    b_f2,
    w_o1,
    b_o1,
    w_o2,
    b_o2,
    w_e1,
    b_e1,
    w_e2,
    species_scale,
    species_shift,
):
    atom_rows, width = features.shape
    slot_count = neighbour.shape[0] // atom_rows
    vmem = pl.BlockSpec(memory_space=pltpu.VMEM)
    lists = (exports_x[0], exports_y[0], exports_z[0])
    ghost_rows = sum(2 * one.shape[1] for one in lists)
    table_rows = atom_rows + ghost_rows
    tiles = atom_rows // LANES
    steps = slot_count // UNROLL * tiles
    ghost_height = sum(2 * packed_height(one.shape[1]) for one in lists)
    packed = packed_height(atom_rows) + ghost_height + 8 * tiles
    lines = math.lcm(slot_count, LANES) // LANES
    inputs = (
        features,
        w_in,
        *lists,
        face_counts,
        displacement,
        neighbour.reshape(-1, LANES),
        neighbour_count,
        species,
        species_scale,
        species_shift,
        w_f1,
        b_f1,
        w_f2,
        w_o1,
        w_o2,
        w_e1.T,
        b_f2,
        b_o1,
        b_o2,
        b_e1,
        w_e2,
    )
    hidden = w_e1.shape[1]
    anywhere = pl.BlockSpec(memory_space=pl.ANY)
    results = (
        jax.ShapeDtypeStruct((9, steps + 1, UNROLL, LANES), F32),
        jax.ShapeDtypeStruct((8, atom_rows), F32),
        jax.ShapeDtypeStruct((8, atom_rows), F32),
        jax.ShapeDtypeStruct((16, atom_rows), F32),
        jax.ShapeDtypeStruct((width, atom_rows), BF16),
        jax.ShapeDtypeStruct((6, width, width), BF16),
        jax.ShapeDtypeStruct((2, hidden, width), BF16),
        jax.ShapeDtypeStruct((2, width, hidden), BF16),
        jax.ShapeDtypeStruct((width, width), F32),
        jax.ShapeDtypeStruct((8, LANES), jnp.int32),
    )
    table_t, rows, order, counts, vals, sorted_t, *weights = pl.pallas_call(
        send_kernel,
        out_shape=(jax.ShapeDtypeStruct((width, table_rows), BF16),) + results,
        in_specs=[anywhere] * len(inputs),
        out_specs=(anywhere,) * (1 + len(results)),
        scratch_shapes=[pltpu.VMEM(one.shape, one.dtype) for one in inputs + results]
        + [
            pltpu.VMEM((width, atom_rows), BF16),
            pltpu.VMEM((width, ghost_rows), BF16),
            pltpu.VMEM((4, lines, LANES, LANES), F32),
            pltpu.VMEM((atom_rows, LANES), F32),
            pltpu.VMEM((8, LANES), jnp.int32),
            pltpu.VMEM((6, 8, LANES), jnp.int32),
            pltpu.SemaphoreType.DMA((len(inputs),)),
            pltpu.SemaphoreType.DMA((1 + len(results),)),
            pltpu.SemaphoreType.DMA((6,)),
            pltpu.SemaphoreType.DMA((6,)),
            pltpu.SemaphoreType.DMA((6,)),
            pltpu.SemaphoreType.DMA((6,)),
        ],
        compiler_params=pltpu.CompilerParams(
            collective_id=0, has_side_effects=True, vmem_limit_bytes=58 * 1024 * 1024
        ),
    )(*inputs)
    span = UNROLL * LANES
    energy, spread = pl.pallas_call(
        functools.partial(pair_kernel, [one.shape[1] for one in lists for _ in range(2)]),
        out_shape=(
            jax.ShapeDtypeStruct((atom_rows,), F32),
            jax.ShapeDtypeStruct((packed, LANES), F32),
        ),
        in_specs=[vmem] * 10 + [pl.BlockSpec(memory_space=pltpu.SMEM)],
        out_specs=(vmem, vmem),
        scratch_shapes=[
            pltpu.VMEM((tiles, width, LANES), F32),
            pltpu.VMEM((tiles, width, LANES), F32),
            pltpu.VMEM((tiles, 8, LANES), F32),
            pltpu.VMEM((steps + 10, width, span), BF16),
            pltpu.VMEM((steps + 10, width, span), BF16),
            pltpu.VMEM((steps + 10, width, span), BF16),
            pltpu.VMEM((steps + 10, RADIAL_ROWS, span), BF16),
            pltpu.VMEM((width, span), BF16),
            pltpu.VMEM((width, span), BF16),
            pltpu.VMEM((width, span), F32),
            pltpu.VMEM((width, span), F32),
            pltpu.VMEM((width, span), F32),
            pltpu.VMEM((width, span), F32),
            pltpu.VMEM((width, span), BF16),
            pltpu.VMEM((width, span), BF16),
            pltpu.VMEM((8, span), F32),
            pltpu.VMEM((8, span), F32),
            pltpu.VMEM((3 * GROUP_ROWS, 128), F32),
            pltpu.VMEM((width, -(-table_rows // CHUNK) * CHUNK + LANES), BF16),
        ],
        compiler_params=pltpu.CompilerParams(vmem_limit_bytes=58 * 1024 * 1024),
        cost_estimate=pl.CostEstimate(
            flops=30_000_000_000, bytes_accessed=4_000_000, transcendentals=16_000_000
        ),
    )(
        rows,
        order,
        counts,
        vals,
        sorted_t,
        table_t,
        *weights,
    )
    last = (spread, order, *lists, face_counts)
    copied = (order, *lists, face_counts)
    forces = pl.pallas_call(
        return_kernel,
        out_shape=jax.ShapeDtypeStruct((3, atom_rows), F32),
        in_specs=[anywhere] * len(last),
        out_specs=vmem,
        scratch_shapes=[pltpu.VMEM(one.shape, one.dtype) for one in copied]
        + [
            pltpu.VMEM((packed, LANES), F32),
            pltpu.VMEM((ghost_height, LANES), F32),
            pltpu.SemaphoreType.DMA((len(last),)),
            pltpu.SemaphoreType.DMA((6,)),
            pltpu.SemaphoreType.DMA((6,)),
        ],
        compiler_params=pltpu.CompilerParams(
            collective_id=1, has_side_effects=True, vmem_limit_bytes=20 * 1024 * 1024
        ),
    )(*last)
    return (energy, forces)


def solution(mesh):
    both = ("geom", "gx", "gy", "gz")
    return jax.shard_map(
        body,
        mesh=mesh,
        in_specs=(
            P(both, None),
            P(None, both),
            P(both),
            P(both),
            P(both),
            P(both, None, None),
            P(both, None, None),
            P(both, None, None),
            P(both, None),
        )
        + (P(),) * 14,
        out_specs=(P(both), P(None, both)),
        check_vma=False,
    )
```

```python
import functools
import math

import jax
import jax.numpy as jnp
from jax import lax
from jax.experimental import pallas as pl
from jax.experimental.pallas import tpu as pltpu
from jax.sharding import PartitionSpec as P

GAMMA = 10.0
CUTOFF = 5.0
LOG_TWO = math.log(2.0)
LOG2E = 1.0 / LOG_TWO
LANES = 128
UNROLL = 4
CHUNK = 256
RADIAL_ROWS = 64
GROUP_ROWS = 32
BEHIND = 2

BF16 = jnp.bfloat16
F32 = jnp.float32


def dot(a, b):
    return jnp.dot(a, b, preferred_element_type=F32)


def dot_nt(a, b):
    return lax.dot_general(a, b, (((1,), (1,)), ((), ())), preferred_element_type=F32)


def split3(value):
    high = value.astype(BF16)
    rest = value - high.astype(F32)
    middle = rest.astype(BF16)
    low = (rest - middle.astype(F32)).astype(BF16)
    return high, middle, low


def split2(value):
    high = value.astype(BF16)
    low = (value - high.astype(F32)).astype(BF16)
    return jnp.concatenate([high, low], axis=0)


def softplus_of(value):
    return jnp.maximum(value, 0.0) + jnp.log(1.0 + jnp.exp(-jnp.abs(value)))


def sigmoid_of(value):
    return 1.0 / (1.0 + jnp.exp(-value))


def one_hot(row, size):
    span = row.shape[1]
    parts = []
    for start in range(0, size, CHUNK):
        spot = jnp.broadcast_to(row - float(start), (16, span)).astype(BF16)
        lanes = lax.broadcasted_iota(jnp.int32, (16, span), 0).astype(F32)
        for b in range(min(CHUNK, size - start) // 16):
            ids = (lanes + float(16 * b)).astype(BF16)
            parts.append(jnp.where(ids == spot, jnp.ones((), BF16), jnp.zeros((), BF16)))
    return jnp.concatenate(parts, axis=0)


def flip(weight):
    return weight.astype(F32).T.astype(BF16)


def packed_height(length):
    return -(-3 * (length // LANES) // 8) * 8


def unpacked(ref, at, length):
    count = length // LANES
    return jnp.concatenate(
        [
            jnp.concatenate(
                [ref[at + c * count + h : at + c * count + h + 1] for h in range(count)], axis=1
            )
            for c in range(3)
        ]
        + [jnp.zeros((5, length), F32)],
        axis=0,
    )


def pair_kernel(
    lengths,
    rows_ref,
    order_ref,
    counts_ref,
    vals_ref,
    feat_ref,
    table_ref,
    square_ref,
    wide_ref,
    tall_ref,
    column_ref,
    held_ref,
    energy_ref,
    spread_ref,
    msg_ref,
    gm_ref,
    own3_ref,
    xj_ref,
    prod_ref,
    sig_ref,
    slope_ref,
    hid_a_ref,
    hid_b_ref,
    filt_a_ref,
    filt_b_ref,
    found_a_ref,
    found_b_ref,
    back_a_ref,
    back_b_ref,
    minus_a_ref,
    minus_b_ref,
    total_ref,
    packed_ref,
):
    width, atoms = feat_ref.shape
    tiles = atoms // LANES
    steps = (rows_ref.shape[1] - 1) // tiles
    span = UNROLL * LANES
    table_rows = table_ref.shape[1]
    idle = tiles * steps

    counts = counts_ref[0:1]
    scale = vals_ref[0:1]
    shift = vals_ref[8:9]
    feat = feat_ref[...].astype(F32)
    row_ref, dist_ref, env_ref, near_ref, far_ref = [rows_ref.at[n] for n in range(5)]

    w2, w2t, wo1, wo1t, wo2, wo2t = [square_ref[n] for n in range(6)]
    w1_back, we1 = wide_ref[0], wide_ref[1]
    w1t, we1t = tall_ref[0], tall_ref[1]
    b_f2, b_o1, b_o2, mu, sharp = [column_ref[:, n : n + 1] for n in range(5)]
    mu, sharp = mu[0:RADIAL_ROWS], sharp[0:RADIAL_ROWS]
    b_e1, w_e2 = [column_ref[0 : we1.shape[0], n : n + 1] for n in (5, 6)]

    def lane_row(ref, at):
        return jnp.concatenate([ref[at, u : u + 1, :] for u in range(UNROLL)], axis=1)

    ends = []
    items = jnp.zeros((), jnp.int32)
    for tile in range(tiles):
        most = jnp.max(counts[:, tile * LANES : (tile + 1) * LANES]).astype(jnp.int32)
        items = items + (most + (UNROLL - 1)) // UNROLL
        ends.append(items)
    rounds = (items + 1) // 2
    turns = (items + 3) // 4

    def place(item):
        tile = jnp.zeros((), jnp.int32)
        first = jnp.zeros((), jnp.int32)
        for end in ends[:-1]:
            past = item >= end
            tile = tile + past.astype(jnp.int32)
            first = jnp.where(past, end, first)
        at = jnp.where((item >= 0) & (item < items), tile * steps + item - first, idle)
        return tile, at

    packed_ref[...] = jnp.zeros_like(packed_ref)
    packed_ref[:, 0:atoms] = table_ref[:, 0:atoms]
    lane_ids = lax.broadcasted_iota(jnp.int32, (width, LANES), 1)
    packed_rows = jnp.full((), atoms, jnp.int32)
    edge = atoms
    for n, length in enumerate(lengths):
        turn = packed_rows & (LANES - 1)
        base = packed_rows - turn
        below = lane_ids < turn
        first = pl.multiple_of(base, LANES)
        last = packed_ref[:, pl.ds(first, LANES)].astype(F32)
        for t in range(length // LANES):
            slab = table_ref[:, edge + t * LANES : edge + (t + 1) * LANES].astype(F32)
            slab = pltpu.roll(slab, turn, 1)
            at = pl.multiple_of(base + t * LANES, LANES)
            packed_ref[:, pl.ds(at, LANES)] = jnp.where(below, last, slab).astype(BF16)
            last = slab
        at = pl.multiple_of(base + length, LANES)
        packed_ref[:, pl.ds(at, LANES)] = jnp.where(below, last, 0.0).astype(BF16)
        packed_rows = packed_rows + held_ref[n, 0]
        edge += length

    def radial_dot(at):
        offset = lane_row(dist_ref, at) - mu
        basis = jnp.exp2(sharp * (offset * offset))
        return (offset * basis).astype(BF16), dot(w1t, basis.astype(BF16))

    def activate(pre):
        grown = jnp.exp2(pre * LOG2E)
        total = 1.0 + grown
        sig = (grown * pl.reciprocal(total, approx=True)).astype(BF16)
        return sig, (jnp.log2(total) - 1.0).astype(BF16)

    def begin(item, hid_ref):
        slope, pre = radial_dot(place(item)[1])
        slope_ref[item + BEHIND] = slope
        sig, hidden = activate(pre)
        sig_ref[item + BEHIND] = sig
        hid_ref[...] = hidden

    def finish(item, filt_ref, found_ref):
        tile, at = place(item)
        prod = found_ref[...] * filt_ref[...]
        prod_ref[item + BEHIND] = prod.astype(BF16)
        weighted = prod * lane_row(env_ref, at)
        part = msg_ref[tile]
        for u in range(UNROLL):
            part = part + weighted[:, u * LANES : (u + 1) * LANES]
        msg_ref[tile] = part

    def forward(size, item, hid_ref, next_ref, filt_ref, found_ref, last_filt_ref, last_found_ref):
        slope, pre = radial_dot(place(item + 1)[1])
        slope_ref[item + BEHIND + 1] = slope
        picked = one_hot(lane_row(rows_ref.at[8], place(item)[1]), size)
        found = dot(packed_ref[:, 0:size], picked)
        filt = dot(w2t, hid_ref[...]) + b_f2
        finish(item - 1, last_filt_ref, last_found_ref)
        sig, hidden = activate(pre)
        sig_ref[item + BEHIND + 1] = sig
        next_ref[...] = hidden
        filt_ref[...] = filt
        found_ref[...] = found
        xj_ref[item + BEHIND] = found.astype(BF16)

    msg_ref[...] = jnp.zeros_like(msg_ref)
    filt_b_ref[...] = jnp.zeros_like(filt_b_ref)
    found_b_ref[...] = jnp.zeros_like(found_b_ref)
    begin(jnp.zeros((), jnp.int32), hid_a_ref)

    def forward_all(size):
        def forward_round(turn, carry):
            a = (filt_a_ref, found_a_ref)
            b = (filt_b_ref, found_b_ref)
            for n in range(0, 4, 2):
                item = 4 * turn + n
                forward(size, item, hid_a_ref, hid_b_ref, *a, *b)
                forward(size, item + 1, hid_b_ref, hid_a_ref, *b, *a)
            return carry

        lax.fori_loop(0, turns, forward_round, 0)

    most = -(-table_rows // CHUNK) * CHUNK
    sizes = [size for size in range(most - 3 * CHUNK, most + 1, CHUNK) if size > 0]
    for n, size in enumerate(sizes):
        fits = packed_rows <= size
        if n:
            fits = fits & (packed_rows > sizes[n - 1])

        @pl.when(fits)
        def _(size=size):
            forward_all(size)

    finish(4 * turns - 1, filt_b_ref, found_b_ref)

    message = jnp.concatenate([msg_ref[t] for t in range(tiles)], axis=1)
    message = (message * LOG_TWO).astype(BF16)
    out_pre = dot(wo1t, message) + b_o1
    out_mid = (softplus_of(out_pre) - LOG_TWO).astype(BF16)
    updated = (feat + dot(wo2t, out_mid) + b_o2).astype(BF16)
    energy_pre = dot(we1, updated) + b_e1
    soft = softplus_of(energy_pre) - LOG_TWO
    energy = scale * jnp.sum(soft * w_e2, axis=0, keepdims=True) + shift
    home = one_hot(order_ref[0:1], atoms)
    plain = dot(split2(jnp.broadcast_to(energy, (8, atoms))), home)
    energy_ref[...] = (plain[0:1] + plain[8:9]).reshape(atoms)
    grad_head = (scale * w_e2 * sigmoid_of(energy_pre)).astype(BF16)
    grad_update = dot(we1t, grad_head).astype(BF16)
    grad_mid = (dot(wo2, grad_update) * sigmoid_of(out_pre)).astype(BF16)
    grad_message = dot(wo1, grad_mid)
    for tile in range(tiles):
        gm_ref[tile] = grad_message[:, tile * LANES : (tile + 1) * LANES]

    total_ref[...] = jnp.zeros_like(total_ref)
    own3_ref[...] = jnp.zeros_like(own3_ref)
    for ref in (back_a_ref, back_b_ref, minus_a_ref, minus_b_ref):
        ref[...] = jnp.zeros_like(ref)
    for early in range(BEHIND):
        prod_ref[early] = jnp.zeros((width, span), BF16)
        slope_ref[early] = jnp.zeros((RADIAL_ROWS, span), BF16)
    for late in range(4):
        ahead = 2 * rounds + BEHIND + late
        xj_ref[ahead] = jnp.zeros((width, span), BF16)
        prod_ref[ahead] = jnp.zeros((width, span), BF16)
        slope_ref[ahead] = jnp.zeros((RADIAL_ROWS, span), BF16)
        sig_ref[ahead] = jnp.zeros((width, span), BF16)

    def pull(item):
        tile, at = place(item)
        grad_b = gm_ref[tile].astype(BF16)
        grad_b_wide = jnp.concatenate([grad_b] * UNROLL, axis=1)
        mixed = dot(w2, grad_b_wide * xj_ref[item + BEHIND])
        return (mixed * sig_ref[item + BEHIND].astype(F32)).astype(BF16)

    def settle(item, grad_pre):
        tile, at = place(item)
        grad_basis = dot(w1_back, grad_pre)
        grad_wide = jnp.concatenate([gm_ref[tile]] * UNROLL, axis=1)
        s1 = jnp.sum(grad_basis * slope_ref[item + BEHIND].astype(F32), axis=0, keepdims=True)
        s2 = jnp.sum(grad_wide * prod_ref[item + BEHIND].astype(F32), axis=0, keepdims=True)
        ratio = s1 * lane_row(near_ref, at) + s2 * lane_row(far_ref, at)
        forces = []
        for c in range(3):
            force = ratio * lane_row(rows_ref.at[5 + c], at)
            part = own3_ref[tile, c : c + 1, :]
            for u in range(UNROLL):
                part = part + force[:, u * LANES : (u + 1) * LANES]
            own3_ref[tile, c : c + 1, :] = part
            forces.append(-force)
        return jnp.concatenate(forces, axis=0)

    def strew(item, minus):
        row = lane_row(row_ref, place(item)[1])
        high = jnp.floor(row * (1.0 / 128))
        low = row - high * 128.0
        wide = (16, span)
        high_b = jnp.broadcast_to(high, wide).astype(BF16)
        low_b = jnp.broadcast_to(low, wide).astype(BF16)
        lanes = lax.broadcasted_iota(jnp.int32, wide, 0).astype(F32)
        ids = [(lanes + float(16 * b)).astype(BF16) for b in range(8)]
        lower = jnp.concatenate(
            [jnp.where(one == low_b, jnp.ones((), BF16), jnp.zeros((), BF16)) for one in ids],
            axis=0,
        )
        here = [ids[b] == high_b for b in range(GROUP_ROWS // 16)]
        placed = []
        for c in range(3):
            part = jnp.broadcast_to(minus[c : c + 1], wide).astype(BF16)
            placed += [jnp.where(mask, part, jnp.zeros((), BF16)) for mask in here]
        return dot_nt(jnp.concatenate(placed, axis=0), lower)

    def backward_round(turn, carry):
        item = 2 * turn
        spread_a = strew(item - 4, minus_a_ref[0:3])
        spread_b = strew(item - 3, minus_b_ref[0:3])
        minus_a = settle(item - 2, back_a_ref[...])
        minus_b = settle(item - 1, back_b_ref[...])
        pull_a = pull(item)
        pull_b = pull(item + 1)
        total_ref[...] = total_ref[...] + spread_a + spread_b
        minus_a_ref[0:3] = minus_a
        minus_b_ref[0:3] = minus_b
        back_a_ref[...] = pull_a
        back_b_ref[...] = pull_b
        return carry

    lax.fori_loop(0, rounds + 2, backward_round, 0)

    spread_ref[...] = jnp.zeros_like(spread_ref)
    group = tiles
    at = 0
    for length in [atoms] + list(lengths):
        count = length // LANES
        first = 0 if at == 0 else group
        for c in range(3):
            rows = total_ref[c * GROUP_ROWS + first : c * GROUP_ROWS + first + count]
            spread_ref[at + c * count : at + (c + 1) * count] = rows
        group = group + count if at else group
        at += packed_height(length)
    for tile in range(tiles):
        spread_ref[at + 8 * tile : at + 8 * tile + 8] = own3_ref[tile]


def neighbours():
    found = []
    for axis in ("gx", "gy", "gz"):
        size = lax.axis_size(axis)
        place = lax.axis_index(axis)
        found.append({axis: lax.rem(place + 1, size)})
        found.append({axis: lax.rem(place + size - 1, size)})
    return found


def greet(found):
    barrier = pltpu.get_barrier_semaphore()
    for device in found:
        pl.semaphore_signal(
            barrier, inc=1, device_id=device, device_id_type=pl.DeviceIdType.MESH
        )
    pl.semaphore_wait(barrier, len(found))


FACES = ((0, 1, 1, 0), (0, 0, 0, 1), (1, 1, 3, 2), (1, 0, 2, 3), (2, 1, 5, 4), (2, 0, 4, 5))


def ready_weights(
    w1_ref,
    b1_ref,
    w2_ref,
    wo1_ref,
    wo2_ref,
    we1_ref,
    bf2_ref,
    bo1_ref,
    bo2_ref,
    be1_ref,
    w_e2_ref,
    square_ref,
    wide_ref,
    tall_ref,
    column_ref,
):
    radial, width = w1_ref.shape
    bias = b1_ref[...].reshape(1, width)
    bias_high = bias.astype(BF16).astype(F32)
    bias_middle = (bias - bias_high).astype(BF16).astype(F32)
    w1 = jnp.concatenate(
        [
            w1_ref[...].astype(F32),
            bias_high,
            bias_middle,
            bias - bias_high - bias_middle,
            jnp.zeros((RADIAL_ROWS - radial - 3, width), F32),
        ],
        axis=0,
    )
    radial_col = lax.broadcasted_iota(jnp.int32, (RADIAL_ROWS, 1), 0)
    tall_ref[0] = w1.T.astype(BF16)
    wide_ref[0] = jnp.where(radial_col < radial, w1, 0.0).astype(BF16)
    wide_ref[1] = we1_ref[...]
    tall_ref[1] = flip(we1_ref[...])
    for n, ref in enumerate((w2_ref, wo1_ref, wo2_ref)):
        square_ref[2 * n] = ref[...]
        square_ref[2 * n + 1] = flip(ref[...])
    ids = lax.broadcasted_iota(jnp.int32, (1, width), 1)
    rows = [
        bf2_ref[...].reshape(1, width) * LOG2E,
        bo1_ref[...].reshape(1, width),
        bo2_ref[...].reshape(1, width),
        ids.astype(F32) * (CUTOFF / (radial - 1)),
        jnp.where(ids < radial, -GAMMA * LOG2E, 0.0),
    ]
    for ref in (be1_ref, w_e2_ref):
        size = ref.shape[0]
        rows.append(
            jnp.concatenate(
                [ref[...].reshape(1, size), jnp.zeros((1, width - size), F32)], axis=1
            )
        )
    rows.append(jnp.zeros((width - len(rows), width), F32))
    column_ref[...] = jnp.concatenate(rows, axis=0).T


def prepare(
    lengths,
    held,
    feat_ref,
    disp_ref,
    index_ref,
    count_ref,
    species_ref,
    scale_ref,
    shift_ref,
    rows_ref,
    order_ref,
    counts_ref,
    vals_ref,
    sorted_ref,
    raw_ref,
    rank_ref,
):
    atoms = feat_ref.shape[0]
    slots = disp_ref.shape[1] // atoms
    tiles = atoms // LANES
    steps = slots // UNROLL
    idle = tiles * steps
    block = math.lcm(slots, LANES)
    lines = block // LANES
    each = block // slots
    groups = atoms // each

    raw_ref[...] = jnp.zeros_like(raw_ref)

    def lay(g, carry):
        for m in range(lines):
            at = pl.multiple_of((g * lines + m) * LANES, LANES)
            three = disp_ref[:, pl.ds(at, LANES)]
            for c in range(3):
                raw_ref[c, m, pl.ds(g, 1), :] = three[c : c + 1]
            line = index_ref[pl.ds(g * lines + m, 1), :]
            raw_ref[3, m, pl.ds(g, 1), :] = line.astype(F32)
        return carry

    lax.fori_loop(0, groups, lay, 0)

    atom_row = lax.broadcasted_iota(jnp.int32, (1, atoms), 1)
    atom_col = lax.broadcasted_iota(jnp.int32, (atoms, 1), 0)
    count_row = count_ref[...].reshape(1, atoms)
    key_row = (count_row * atoms - atom_row).astype(F32)
    count_col = jnp.broadcast_to(count_row.astype(F32), (128, atoms)).T[:, 0:1]
    key_col = count_col * float(atoms) - atom_col.astype(F32)
    rank_col = jnp.sum(jnp.where(key_row > key_col, 1.0, 0.0), axis=1, keepdims=True)
    perm = jnp.where(rank_col == atom_row.astype(F32), 1.0, 0.0).astype(BF16)

    rank_ref[...] = jnp.broadcast_to(rank_col, (atoms, LANES))
    order_ref[...] = rank_ref[...].T[0:8]
    lane_ids = lax.broadcasted_iota(jnp.int32, (groups, LANES), 1).astype(F32)
    blocks = []
    for a in range(each):
        rank = rank_ref[pl.ds(a, groups, stride=each), :]
        blocks.append(
            jnp.concatenate(
                [
                    jnp.where(rank - float(t * LANES) == lane_ids, 1.0, 0.0).astype(BF16)
                    for t in range(tiles)
                ],
                axis=1,
            )
        )
        if groups < LANES:
            blocks.append(jnp.zeros((LANES - groups, atoms), BF16))
    spots = jnp.concatenate(blocks, axis=0)

    def columns(c):
        turned = jnp.concatenate([raw_ref[c, m].T for m in range(lines)], axis=0)
        return jnp.concatenate(
            [turned[a * slots : (a + 1) * slots] for a in range(each)], axis=1
        )

    def put(ref, value):
        for tile in range(tiles):
            for s in range(steps):
                ref[tile * steps + s] = value[
                    s * UNROLL : (s + 1) * UNROLL, tile * LANES : (tile + 1) * LANES
                ]
        ref[idle] = jnp.zeros((UNROLL, LANES), F32)

    raw = jnp.concatenate([columns(c) for c in range(3)], axis=0)
    index = columns(3)
    index_high = jnp.floor(index * (1.0 / 128))
    index_low = index - index_high * 128.0
    stack = jnp.concatenate(
        list(split3(raw)) + [index_high.astype(BF16), index_low.astype(BF16)], axis=0
    )
    found = dot(stack, spots)
    size = 3 * slots
    disp = found[0:size] + found[size : 2 * size] + found[2 * size : 3 * size]
    row = found[3 * size : 3 * size + slots] * 128.0 + found[3 * size + slots : 3 * size + 2 * slots]
    put(rows_ref.at[0], row)
    packed = row
    edge = atoms
    for length, used in zip(lengths[:-1], held):
        edge += length
        packed = packed - jnp.where(row >= float(edge), float(length) - used.astype(F32), 0.0)
    put(rows_ref.at[8], packed)
    counts8 = dot(jnp.broadcast_to(count_row, (8, atoms)).astype(F32).astype(BF16), perm)
    counts = counts8[0:1]
    counts_ref[...] = counts8
    kinds = scale_ref.shape[0]
    kind_ids = lax.broadcasted_iota(jnp.int32, (kinds, 1), 0)
    kind_pick = jnp.where(kind_ids == species_ref[...].reshape(1, atoms), 1.0, 0.0).astype(BF16)
    pair_of = jnp.concatenate(
        [
            jnp.broadcast_to(scale_ref[...].reshape(1, kinds), (8, kinds)),
            jnp.broadcast_to(shift_ref[...].reshape(1, kinds), (8, kinds)),
        ],
        axis=0,
    )
    atom_vals = sum(dot(part, kind_pick) for part in split3(pair_of))
    vals_ref[...] = sum(dot(part, perm) for part in split3(atom_vals))
    sorted_ref[...] = dot(feat_ref[...].astype(F32).T.astype(BF16), perm).astype(BF16)

    dx = disp[0:slots]
    dy = disp[slots : 2 * slots]
    dz = disp[2 * slots : 3 * slots]
    squared = dx * dx + dy * dy + dz * dz
    distance = jnp.sqrt(squared)
    put(rows_ref.at[1], distance)
    slot_ids = lax.broadcasted_iota(jnp.int32, (slots, 1), 0).astype(F32)
    live = jnp.where(slot_ids < counts, 1.0, 0.0)
    y = (math.pi / CUTOFF) * distance - 0.5 * math.pi
    y2 = y * y
    sin_y = y * (
        1.0
        + y2
        * (
            -1.0 / 6
            + y2 * (1.0 / 120 + y2 * (-1.0 / 5040 + y2 * (1.0 / 362880 - y2 * (1.0 / 39916800))))
        )
    )
    envelope = (0.5 - 0.5 * sin_y) * live
    put(rows_ref.at[2], envelope)
    cos_y = 1.0 + y2 * (
        -0.5
        + y2
        * (
            1.0 / 24
            + y2
            * (
                -1.0 / 720
                + y2 * (1.0 / 40320 + y2 * (-1.0 / 3628800 + y2 * (1.0 / 479001600)))
            )
        )
    )
    inverse = live / distance
    put(rows_ref.at[3], envelope * (-2.0 * GAMMA) * inverse)
    put(rows_ref.at[4], (-0.5 * math.pi / CUTOFF * LOG_TWO) * cos_y * inverse)
    put(rows_ref.at[5], dx)
    put(rows_ref.at[6], dy)
    put(rows_ref.at[7], dz)


INPUTS = 23
OUTPUTS = 10


def named_faces(lists, used_ref):
    found = []
    used = used_ref[...]
    for dim, side, column, _ in FACES:
        names = lists[dim][side : side + 1, :]
        lanes = lax.broadcasted_iota(jnp.int32, names.shape, 1)
        found.append(jnp.where(lanes < used[:, column : column + 1], names, -1).astype(F32))
    return found


def send_kernel(*refs):
    far, refs = refs[:INPUTS], refs[INPUTS:]
    table_ref, results, refs = refs[0], refs[1 : OUTPUTS + 1], refs[OUTPUTS + 1 :]
    near, made, refs = refs[:INPUTS], refs[INPUTS : INPUTS + OUTPUTS], refs[INPUTS + OUTPUTS :]
    mine_ref, stage_ref, raw_ref, rank_ref, tag_ref, tags_ref, *sems = refs
    load_sem, save_sem, send_sem, recv_sem, tag_send_sem, tag_recv_sem = sems
    loads = [
        pltpu.make_async_copy(one, two, load_sem.at[n])
        for n, (one, two) in enumerate(zip(far, near))
    ]
    for load in loads:
        load.start()
    found = neighbours()
    greet(found)
    feat_ref, w_ref = near[0:2]
    used_here = near[5]
    atoms = feat_ref.shape[0]
    for load in loads[0:6]:
        load.wait()
    used = used_here[...]
    faces = used.shape[1]
    tag = jnp.concatenate([used, jnp.zeros((1, LANES - faces), jnp.int32)], axis=1)
    tag_ref[...] = jnp.broadcast_to(tag, tag_ref.shape)
    tags = []
    for n in range(faces):
        tag = pltpu.make_async_remote_copy(
            src_ref=tag_ref,
            dst_ref=tags_ref.at[n],
            send_sem=tag_send_sem.at[n],
            recv_sem=tag_recv_sem.at[n],
            device_id=found[n],
            device_id_type=pl.DeviceIdType.MESH,
        )
        tag.start()
        tags.append(tag)
    x_t = dot(feat_ref[...], w_ref[...]).T.astype(BF16)
    copies = []
    start = 0
    for n, names in enumerate(named_faces(near[2:5], near[5])):
        length = names.shape[1]
        stage_ref[:, start : start + length] = dot(x_t, one_hot(names, atoms)).astype(BF16)
        copy = pltpu.make_async_remote_copy(
            src_ref=stage_ref.at[:, pl.ds(start, length)],
            dst_ref=table_ref.at[:, pl.ds(atoms + start, length)],
            send_sem=send_sem.at[n],
            recv_sem=recv_sem.at[n],
            device_id=found[n],
            device_id_type=pl.DeviceIdType.MESH,
        )
        copy.start()
        copies.append(copy)
        start += length
    mine_ref[...] = x_t
    saves = [pltpu.make_async_copy(mine_ref, table_ref.at[:, pl.ds(0, atoms)], save_sem.at[0])]
    saves[0].start()
    for load in loads[6:]:
        load.wait()
    rows_ref, order_ref, counts_ref, vals_ref, sorted_ref = made[0:5]
    for tag in tags:
        tag.wait()
    held = [tags_ref[n, 0:1, face[2] : face[2] + 1] for n, face in enumerate(FACES)]
    made[-1][...] = jnp.concatenate(
        [jnp.broadcast_to(one, (1, LANES)) for one in held]
        + [jnp.zeros((8 - faces, LANES), jnp.int32)],
        axis=0,
    )
    lengths = [near[2 + face[0]].shape[1] for face in FACES]
    prepare(
        lengths,
        held,
        feat_ref,
        *near[6:12],
        rows_ref,
        order_ref,
        counts_ref,
        vals_ref,
        sorted_ref,
        raw_ref,
        rank_ref,
    )
    ready_weights(*near[12:], *made[5:9])
    for n, (one, two) in enumerate(zip(made, results)):
        save = pltpu.make_async_copy(one, two, save_sem.at[n + 1])
        save.start()
        saves.append(save)
    for copy in saves + copies:
        copy.wait()


def return_kernel(
    spread_ref,
    order_ref,
    ex_ref,
    ey_ref,
    ez_ref,
    used_ref,
    force_ref,
    order_here,
    ex_here,
    ey_here,
    ez_here,
    used_here,
    mine_ref,
    land_ref,
    load_sem,
    send_sem,
    recv_sem,
):
    atoms = force_ref.shape[1]
    pairs = (
        (spread_ref, mine_ref),
        (order_ref, order_here),
        (ex_ref, ex_here),
        (ey_ref, ey_here),
        (ez_ref, ez_here),
        (used_ref, used_here),
    )
    loads = [
        pltpu.make_async_copy(one, two, load_sem.at[n]) for n, (one, two) in enumerate(pairs)
    ]
    for load in loads:
        load.start()
    lists = (ex_here, ey_here, ez_here)
    found = neighbours()
    greet(found)
    base = packed_height(atoms)
    places = []
    copies = []
    start = 0
    for n, (dim, _, _, to) in enumerate(FACES):
        places.append((start, lists[dim].shape[1]))
        length = packed_height(lists[dim].shape[1])
        copy = pltpu.make_async_remote_copy(
            src_ref=spread_ref.at[pl.ds(base + start, length)],
            dst_ref=land_ref.at[pl.ds(start, length)],
            send_sem=send_sem.at[n],
            recv_sem=recv_sem.at[n],
            device_id=found[to ^ 1],
            device_id_type=pl.DeviceIdType.MESH,
        )
        copy.start()
        copies.append(copy)
        start += length
    for load in loads:
        load.wait()
    picks = jnp.concatenate(
        [one_hot(names, atoms) for names in named_faces(lists, used_here)], axis=1
    )
    total = unpacked(mine_ref, 0, atoms)
    own = base + start
    own = [mine_ref[own + 8 * t : own + 8 * t + 8] for t in range(atoms // LANES)]
    part = dot(split2(jnp.concatenate(own, axis=1)), one_hot(order_here[0:1], atoms))
    total = total + part[0:8] + part[8:16]
    for copy in copies:
        copy.wait()
    values = jnp.concatenate([unpacked(land_ref, *place) for place in places], axis=1)
    part = dot_nt(split2(values), picks)
    total = total + part[0:8] + part[8:16]
    force_ref[...] = total[0:3]


def body(
    features,
    displacement,
    neighbour,
    neighbour_count,
    species,
    exports_x,
    exports_y,
    exports_z,
    face_counts,
    w_in,
    w_f1,
    b_f1,
    w_f2,
    b_f2,
    w_o1,
    b_o1,
    w_o2,
    b_o2,
    w_e1,
    b_e1,
    w_e2,
    species_scale,
    species_shift,
):
    atom_rows, width = features.shape
    slot_count = neighbour.shape[0] // atom_rows
    vmem = pl.BlockSpec(memory_space=pltpu.VMEM)
    lists = (exports_x[0], exports_y[0], exports_z[0])
    ghost_rows = sum(2 * one.shape[1] for one in lists)
    table_rows = atom_rows + ghost_rows
    tiles = atom_rows // LANES
    steps = slot_count // UNROLL * tiles
    ghost_height = sum(2 * packed_height(one.shape[1]) for one in lists)
    packed = packed_height(atom_rows) + ghost_height + 8 * tiles
    lines = math.lcm(slot_count, LANES) // LANES
    inputs = (
        features,
        w_in,
        *lists,
        face_counts,
        displacement,
        neighbour.reshape(-1, LANES),
        neighbour_count,
        species,
        species_scale,
        species_shift,
        w_f1,
        b_f1,
        w_f2,
        w_o1,
        w_o2,
        w_e1.T,
        b_f2,
        b_o1,
        b_o2,
        b_e1,
        w_e2,
    )
    hidden = w_e1.shape[1]
    anywhere = pl.BlockSpec(memory_space=pl.ANY)
    results = (
        jax.ShapeDtypeStruct((9, steps + 1, UNROLL, LANES), F32),
        jax.ShapeDtypeStruct((8, atom_rows), F32),
        jax.ShapeDtypeStruct((8, atom_rows), F32),
        jax.ShapeDtypeStruct((16, atom_rows), F32),
        jax.ShapeDtypeStruct((width, atom_rows), BF16),
        jax.ShapeDtypeStruct((6, width, width), BF16),
        jax.ShapeDtypeStruct((2, hidden, width), BF16),
        jax.ShapeDtypeStruct((2, width, hidden), BF16),
        jax.ShapeDtypeStruct((width, width), F32),
        jax.ShapeDtypeStruct((8, LANES), jnp.int32),
    )
    table_t, rows, order, counts, vals, sorted_t, *weights = pl.pallas_call(
        send_kernel,
        out_shape=(jax.ShapeDtypeStruct((width, table_rows), BF16),) + results,
        in_specs=[anywhere] * len(inputs),
        out_specs=(anywhere,) * (1 + len(results)),
        scratch_shapes=[pltpu.VMEM(one.shape, one.dtype) for one in inputs + results]
        + [
            pltpu.VMEM((width, atom_rows), BF16),
            pltpu.VMEM((width, ghost_rows), BF16),
            pltpu.VMEM((4, lines, LANES, LANES), F32),
            pltpu.VMEM((atom_rows, LANES), F32),
            pltpu.VMEM((8, LANES), jnp.int32),
            pltpu.VMEM((6, 8, LANES), jnp.int32),
            pltpu.SemaphoreType.DMA((len(inputs),)),
            pltpu.SemaphoreType.DMA((1 + len(results),)),
            pltpu.SemaphoreType.DMA((6,)),
            pltpu.SemaphoreType.DMA((6,)),
            pltpu.SemaphoreType.DMA((6,)),
            pltpu.SemaphoreType.DMA((6,)),
        ],
        compiler_params=pltpu.CompilerParams(
            collective_id=0, has_side_effects=True, vmem_limit_bytes=58 * 1024 * 1024
        ),
    )(*inputs)
    span = UNROLL * LANES
    energy, spread = pl.pallas_call(
        functools.partial(pair_kernel, [one.shape[1] for one in lists for _ in range(2)]),
        out_shape=(
            jax.ShapeDtypeStruct((atom_rows,), F32),
            jax.ShapeDtypeStruct((packed, LANES), F32),
        ),
        in_specs=[vmem] * 10 + [pl.BlockSpec(memory_space=pltpu.SMEM)],
        out_specs=(vmem, vmem),
        scratch_shapes=[
            pltpu.VMEM((tiles, width, LANES), F32),
            pltpu.VMEM((tiles, width, LANES), F32),
            pltpu.VMEM((tiles, 8, LANES), F32),
            pltpu.VMEM((steps + 10, width, span), BF16),
            pltpu.VMEM((steps + 10, width, span), BF16),
            pltpu.VMEM((steps + 10, width, span), BF16),
            pltpu.VMEM((steps + 10, RADIAL_ROWS, span), BF16),
            pltpu.VMEM((width, span), BF16),
            pltpu.VMEM((width, span), BF16),
            pltpu.VMEM((width, span), F32),
            pltpu.VMEM((width, span), F32),
            pltpu.VMEM((width, span), F32),
            pltpu.VMEM((width, span), F32),
            pltpu.VMEM((width, span), BF16),
            pltpu.VMEM((width, span), BF16),
            pltpu.VMEM((8, span), F32),
            pltpu.VMEM((8, span), F32),
            pltpu.VMEM((3 * GROUP_ROWS, 128), F32),
            pltpu.VMEM((width, -(-table_rows // CHUNK) * CHUNK + LANES), BF16),
        ],
        compiler_params=pltpu.CompilerParams(vmem_limit_bytes=58 * 1024 * 1024),
        cost_estimate=pl.CostEstimate(
            flops=30_000_000_000, bytes_accessed=4_000_000, transcendentals=16_000_000
        ),
    )(
        rows,
        order,
        counts,
        vals,
        sorted_t,
        table_t,
        *weights,
    )
    last = (spread, order, *lists, face_counts)
    copied = (order, *lists, face_counts)
    forces = pl.pallas_call(
        return_kernel,
        out_shape=jax.ShapeDtypeStruct((3, atom_rows), F32),
        in_specs=[anywhere] * len(last),
        out_specs=vmem,
        scratch_shapes=[pltpu.VMEM(one.shape, one.dtype) for one in copied]
        + [
            pltpu.VMEM((packed, LANES), F32),
            pltpu.VMEM((ghost_height, LANES), F32),
            pltpu.SemaphoreType.DMA((len(last),)),
            pltpu.SemaphoreType.DMA((6,)),
            pltpu.SemaphoreType.DMA((6,)),
        ],
        compiler_params=pltpu.CompilerParams(
            collective_id=1, has_side_effects=True, vmem_limit_bytes=20 * 1024 * 1024
        ),
    )(*last)
    return (energy, forces)


def solution(mesh):
    both = ("geom", "gx", "gy", "gz")
    return jax.shard_map(
        body,
        mesh=mesh,
        in_specs=(
            P(both, None),
            P(None, both),
            P(both),
            P(both),
            P(both),
            P(both, None, None),
            P(both, None, None),
            P(both, None, None),
            P(both, None),
        )
        + (P(),) * 14,
        out_specs=(P(both), P(None, both)),
        check_vma=False,
    )
```
